512 devices in a mesh: dp: 4 (over y), vocab: 128 (over z, x, core).
Axes of the slice: x: 4, y: 4, z: 16, core: 2. Of those that a mesh axis runs over, the one named last changes fastest.
Arguments:
- hidden: bfloat16 [512, 4096], P('dp'), may hold values from -32 to 32
- head_weight: bfloat16 [4096, 151936], P('dp', 'vocab'), may hold values from -0.5 to 0.5
- frozen_logits: bfloat16 [512, 151936], P('dp', 'vocab'), may hold values from -9 to 15
- frozen_norms: float32 [512], P('dp'), may hold values from 9 to 27, as said below
- advantages: float32 [512], P('dp'), may hold values from -4 to 4
- ratios: float32 [512], P('dp'), may hold values from 0.6 to 1.45
- target_tokens: int32 [512], P('dp'), may hold values from 0 to 151935, as said below
- counted: int32 [512], P('dp'), may hold values from 0 to 1, as said below
Outputs:
- grad_hidden: bfloat16 [512, 4096], P(None, ('dp', 'vocab'))
- grad_head: bfloat16 [4096, 151936], P('dp', 'vocab')
- divergence: float32 [512], P('dp')
The draws below stay inside these ranges and needn't reach their ends.
Inputs may be any that keep to these rules, and one draw needn't show every extreme that they name: `frozen_norms`: each token's log-sum-exp of frozen_logits over the vocabulary, taken in float32. `target_tokens`: ids of the vocabulary; the last token's target is the end token, id 151936 - 1. 1 marks a counted token; the last token is always counted.
All inputs are finite; a program needn't handle non-finite values.
Results may differ from the reference program's by a relative error of at most 0.0049.
Values may be sent and summed in bfloat16 or wider, within the bound.
A program may use at most 64 MiB of HBM per device.

```python
import math
import jax
import jax.numpy as jnp
from jax import lax

D = 4096
VOCAB = 151936
TOKENS = 512


favored_count = 64


def column_factor(column):
    return 0.5 + 1.1 * column.astype(jnp.float32) / VOCAB


def column_of(key, column):
    raw = jnp.clip(jax.random.normal(jax.random.fold_in(key, column), (D,), jnp.float32), -6.0, 6.0)
    return raw * column_factor(column) / math.sqrt(D)


def favored_set(key):
    picks = jax.random.randint(jax.random.fold_in(key, 700031), (TOKENS, favored_count), 0, VOCAB)
    positions = jnp.arange(TOKENS, dtype=jnp.int32)
    slots = jnp.arange(favored_count, dtype=jnp.int32)
    ending = (positions == TOKENS - 1)[:, None] & (slots == 0)[None, :]
    return jnp.where(ending, VOCAB - 1, picks).astype(jnp.int32)


def drawn_rows(key, favored):
    levels = 14.0 - 7.0 * jnp.arange(favored_count, dtype=jnp.float32) / favored_count

    def one_row(columns):
        stack = jax.vmap(lambda column: column_of(key, column))(columns)
        factor = column_factor(columns)
        return jnp.sum(stack * (levels / (factor * factor))[:, None], axis=0)
    return lax.map(one_row, favored)


def frozen_table(key, normal_scale):
    favored = favored_set(key)
    key = jax.random.fold_in(key, 700041)
    key_base = jax.random.fold_in(key, 0)
    key_jitter = jax.random.fold_in(key, 2)
    base = normal_scale * jax.random.normal(key_base, (TOKENS, VOCAB), jnp.float32)
    base = jnp.clip(base, -9.0, 9.0)
    jitter = normal_scale * jax.random.normal(key_jitter, (TOKENS, favored_count), jnp.float32)
    jitter = jnp.clip(jitter, -3.0, 3.0)
    levels = 12.0 - 6.0 * jnp.arange(favored_count, dtype=jnp.float32) / favored_count
    planted = levels[None, :] + jitter
    rows = jnp.broadcast_to(jnp.arange(TOKENS, dtype=jnp.int32)[:, None], (TOKENS, favored_count))
    table = base.at[rows, favored].max(planted)
    return table.astype(jnp.bfloat16)


def draw_head_weight(key, part):
    columns = jnp.arange(VOCAB, dtype=jnp.int32)
    matrix = jax.vmap(lambda column: column_of(key, column), out_axes=1)(columns)
    return matrix.astype(jnp.bfloat16)


def draw_hidden(key, part):
    base_key = key
    favored = favored_set(base_key)
    planted = drawn_rows(base_key, favored)
    key = jax.random.fold_in(key, 700011)
    key_rows = jax.random.fold_in(key, 0)
    values = jnp.clip(jax.random.normal(key_rows, (TOKENS, D), jnp.float32), -6.0, 6.0) + planted
    return jnp.clip(values, -32.0, 32.0).astype(jnp.bfloat16)


def draw_frozen_logits(key, part):
    table = frozen_table(key, 1.5)
    return table


def draw_frozen_norms(key, part):
    table = frozen_table(key, 1.5)
    values = table.astype(jnp.float32)
    largest = jnp.max(values, axis=1)
    return largest + jnp.log(jnp.sum(jnp.exp(values - largest[:, None]), axis=1))


def draw_target_tokens(key, part):
    favored = favored_set(key)
    key = jax.random.fold_in(key, 700051)
    key_kind, key_slot, key_wide, key_any = jax.random.split(key, 4)
    kind = jax.random.randint(key_kind, (TOKENS,), 0, 16)
    near = jax.random.randint(key_slot, (TOKENS,), 0, 8)
    wide = jax.random.randint(key_wide, (TOKENS,), 0, favored_count)
    slot = jnp.where(kind < 11, near, wide).astype(jnp.int32)
    chosen = jnp.take_along_axis(favored, slot[:, None], axis=1)[:, 0]
    anywhere = jax.random.randint(key_any, (TOKENS,), 0, VOCAB)
    targets = jnp.where(kind == 15, anywhere, chosen)
    positions = jnp.arange(TOKENS, dtype=jnp.int32)
    return jnp.where(positions == TOKENS - 1, VOCAB - 1, targets).astype(jnp.int32)


def draw_counted(key, part):
    key = jax.random.fold_in(key, 700023)
    positions = jnp.arange(TOKENS, dtype=jnp.int32)
    chance = 150 + 750 * positions // TOKENS
    picked = (jax.random.randint(key, (TOKENS,), 0, 1000) < chance).astype(jnp.int32)
    return jnp.where(positions == TOKENS - 1, 1, picked).astype(jnp.int32)


def steps_of(stream_key, extent, cuts, low, high):
    level, own = 1.0, jax.random.fold_in(stream_key, 6)
    for position, parts in cuts:
        steps = jnp.exp(jax.random.uniform(jax.random.fold_in(own, position), (parts,), jnp.float32, low / len(cuts), high / len(cuts)))
        level = level * jnp.repeat(steps, extent[position] // parts).reshape([-1 if axis == position else 1 for axis in range(len(extent))])
    return level


def noise(rng, shape, width, limit, pieces=(), held_as=jnp.bfloat16):
    entries = jax.random.normal(rng, shape, jnp.float32) * width
    if len(pieces) > 0:
        entries = steps_of(rng, shape, pieces, -0.22, 0.18) * entries
    return jnp.clip(entries, min=-limit, max=limit).astype(held_as)


def setup_inputs(seed: int = 0) -> dict:
    splits = jax.random.split(jax.random.key(seed), 9)
    hidden = draw_hidden(jax.random.fold_in(splits[8], 71), 0)
    head_weight = draw_head_weight(jax.random.fold_in(splits[8], 71), 0)
    frozen_logits = draw_frozen_logits(jax.random.fold_in(splits[8], 71), 0)
    frozen_norms = draw_frozen_norms(jax.random.fold_in(splits[8], 71), 0)
    advantages = noise(splits[4], (TOKENS,), 1.0, 4.0, ((0, 4),), jnp.float32)
    ratios = jnp.clip(0.6 + 0.85 * jax.random.uniform(splits[5], (TOKENS,), jnp.float32) ** steps_of(splits[5], (TOKENS,), ((0, 4),), -0.2, 0.2), 0.6, 1.45)
    target_tokens = draw_target_tokens(jax.random.fold_in(splits[8], 71), 0)
    counted = draw_counted(jax.random.fold_in(splits[8], 71), 0)
    return {"hidden": hidden, "head_weight": head_weight, "frozen_logits": frozen_logits, "frozen_norms": frozen_norms, "advantages": advantages, "ratios": ratios, "target_tokens": target_tokens, "counted": counted}


clip_eps = 0.2
penalty = 0.1


def reference(hidden, head_weight, frozen_logits, frozen_norms, advantages, ratios, target_tokens, counted):
    logits = jnp.dot(hidden, head_weight, preferred_element_type=jnp.float32)
    frozen = frozen_logits.astype(jnp.float32)
    row_top = jnp.max(logits, axis=1, keepdims=True)
    shifted = jnp.exp(logits - row_top)
    row_total = jnp.sum(shifted, axis=1, keepdims=True)
    row_cross = jnp.sum(shifted * (logits - frozen), axis=1, keepdims=True)
    divergence = row_cross[:, 0] / row_total[:, 0] - row_top[:, 0] - jnp.log(row_total[:, 0]) + frozen_norms
    probabilities = shifted / row_total
    mask_values = counted.astype(jnp.float32)
    weight = mask_values / jnp.sum(mask_values)
    active = jnp.where(advantages >= 0.0, ratios <= 1.0 + clip_eps, ratios >= 1.0 - clip_eps)
    policy = jnp.where(active, -advantages * ratios, jnp.zeros_like(ratios))
    onehot = (target_tokens[:, None] == jnp.arange(VOCAB, dtype=jnp.int32)[None, :]).astype(jnp.float32)
    grad_logits = weight[:, None] * (policy[:, None] * (onehot - probabilities)
                                     + penalty * probabilities * (logits - frozen - row_cross / row_total))
    grad_logits = grad_logits.astype(jnp.bfloat16)
    grad_hidden = jnp.dot(grad_logits, head_weight.T, preferred_element_type=jnp.float32).astype(jnp.bfloat16)
    grad_head = jnp.dot(hidden.T, grad_logits, preferred_element_type=jnp.float32).astype(jnp.bfloat16)
    return grad_hidden, grad_head, divergence
```

```python
import functools

import jax
import jax.numpy as jnp
from jax import lax
from jax.experimental import pallas as pl
from jax.experimental.pallas import tpu as pltpu
from jax.sharding import PartitionSpec as P

clip_eps = 0.2
penalty = 0.1

NX = 4
HALF = 608
PIECES = ((0, 320), (320, 288))
SENT = (608, 592)
ROWS = 2 * HALF
DEEP = 1280
ONE = 512.0
TWO = 256.0
MESH = pl.DeviceIdType.MESH
F32 = jnp.float32
BF16 = jnp.bfloat16


def pack(values, scale):
    top = 8388607.0
    whole = jnp.clip(jnp.floor(values * scale + 0.5), -top, top).astype(jnp.int32)
    quarter = values.shape[0] // 4
    a, b, c, d = (whole[k * quarter : (k + 1) * quarter] for k in range(4))
    low = 0xFFFFFF
    return (
        (a & low) | (d << 24),
        (b & low) | ((d >> 8) << 24),
        (c & low) | ((d >> 16) << 24),
    )


def unpack(u, v, w, scale):
    parts = [(word << 8) >> 8 for word in (u, v, w)]
    parts.append(((u >> 24) & 0xFF) | (((v >> 24) & 0xFF) << 8) | ((w >> 24) << 16))
    back = 1.0 / scale
    return [part.astype(F32) * back for part in parts]


def kernel(
    devices,
    hidden, head, frozen, norms, advantages, ratios, targets, counted,
    out_hidden, out_head, out_div,
    head_v, head_t, tail, frozen_v, frozen_f, hid, via, logits, hold,
    snd2, snd1, snd3, rcv2, rcv1, rcv3,
    cnt, cnt_in, st1, st1_in, st2, st2_in,
    g, prod, prod_in, mid, xs, xs_in, zs, zs_in, total_h, head_o,
    load_sem, h_send, h_recv, sh_send, sh_recv, r_send, r_recv,
    c_send, c_recv, s1_send, s1_recv, s2_send, s2_recv,
    g_send, g_recv, a_send, a_recv, x_send, x_recv, z_send, z_recv, o_sem,
):
    NZ = devices // (2 * NX)
    GROUP = 2 * NX
    width = hid.shape[2]
    vocab_here = head.shape[0]
    me = lax.axis_index("dp")
    v = lax.axis_index("vocab")
    core = lax.rem(v, 2)
    x = lax.rem(v // 2, NX)
    z = v // GROUP
    xc = lax.rem(v, GROUP)
    right, far, left = (lax.rem(me + k, 4) for k in (1, 2, 3))
    sibling = (me, v + 1 - 2 * core)

    def in_group(k):
        return (me, z * GROUP + lax.rem(xc + k, GROUP))

    def along_x(k):
        return (me, z * GROUP + lax.rem(x + k, NX) * 2 + core)

    def along_z(k):
        return (me, lax.rem(z + k, NZ) * GROUP + xc)

    def remote(src, dst, send, recv, device):
        return pltpu.make_async_remote_copy(
            src_ref=src, dst_ref=dst, send_sem=send, recv_sem=recv,
            device_id=device, device_id_type=MESH,
        )

    def lanes(block):
        return pl.ds(pl.multiple_of(block * width, width), width)

    half_tok = hid.shape[1] // 2
    mine = pl.ds(pl.multiple_of(core * half_tok, half_tok), half_tok)

    load_head = pltpu.make_async_copy(head, head_v, load_sem.at[0])
    load_own = pltpu.make_async_copy(hidden.at[:, lanes(me)], hid.at[0], load_sem.at[1])
    load_frozen = pltpu.make_async_copy(frozen, frozen_v, load_sem.at[2])
    barrier = pltpu.get_barrier_semaphore()
    for k in (1, 2, 3):
        pl.semaphore_signal(barrier, inc=1, device_id=(lax.rem(me + k, 4), v), device_id_type=MESH)
    for k in range(1, GROUP):
        pl.semaphore_signal(barrier, inc=1, device_id=in_group(k), device_id_type=MESH)

    def greet(k, carry):
        pl.semaphore_signal(barrier, inc=1, device_id=along_z(k), device_id_type=MESH)
        return carry

    lax.fori_loop(1, NZ, greet, 0)
    load_head.start()
    load_own.start()
    load_frozen.start()
    cnt[...] = counted[...].astype(F32)
    pl.semaphore_wait(barrier, 3 + (GROUP - 1) + (NZ - 1))

    onward = (lax.rem(me + 1 + 2 * core, 4), v)
    h_right = remote(hidden.at[mine, lanes(right)], hid.at[3, mine], h_send.at[0], h_recv.at[0], (right, v))
    h_left = remote(hidden.at[mine, lanes(left)], hid.at[1, mine], h_send.at[1], h_recv.at[1], (left, v))
    h_far = remote(hidden.at[mine, lanes(far)], via, h_send.at[2], h_recv.at[2], onward)
    h_on = remote(via, hid.at[2, mine], h_send.at[3], h_recv.at[3], onward)
    h_right.start()
    h_left.start()
    h_far.start()
    counts = [
        remote(cnt, cnt_in.at[k - 1], c_send.at[k - 1], c_recv.at[k - 1], (lax.rem(me + k, 4), v))
        for k in (1, 2, 3)
    ]
    for copy in counts:
        copy.start()
    share = {
        r: remote(hid.at[r, mine], hid.at[r, mine], sh_send.at[r], sh_recv.at[r], sibling)
        for r in (1, 2, 3)
    }

    for r in range(4):
        g[r, pl.ds(1184, DEEP - 1184)] = jnp.zeros((DEEP - 1184, g.shape[2]), BF16)
    load_head.wait()

    def product(r, start, size):
        valid = min(size, vocab_here - start)
        rows = head_v[pl.ds(start, valid)]
        return valid, lax.dot_general(
            rows, hid[r], (((1,), (1,)), ((), ())), preferred_element_type=F32
        )

    def put(dst, at, r, start, size):
        valid, value = product(r, start, size)
        if valid < size:
            floor = valid // 8 * 8
            dst[pl.ds(at + floor, size - floor)] = jnp.zeros((size - floor, value.shape[1]), F32)
        dst[pl.ds(at, valid)] = value

    def send_packed(buffer, slot, piece, values, scale):
        at, size = PIECES[piece]
        quarter, at = size // 4, at // 4 * 3
        for k, words in enumerate(pack(values, scale)):
            buffer[slot, pl.ds(at + k * quarter, quarter)] = words

    def read_packed(buffer, slot, piece, scale):
        at, size = PIECES[piece]
        quarter, at = size // 4, at // 4 * 3
        return unpack(*(buffer[slot, pl.ds(at + k * quarter, quarter)] for k in range(3)), scale)

    def packed_copy(step, slot, piece):
        snd, rcv = ((snd2, rcv2), (snd1, rcv1), (snd3, rcv3))[step]
        at, size = PIECES[piece]
        rows = pl.ds(at // 4 * 3, size // 4 * 3)
        sem = (step * 2 + slot) * 2 + piece
        return remote(
            snd.at[slot, rows], rcv.at[slot, rows], r_send.at[sem], r_recv.at[sem],
            ((right, left)[slot], v),
        )

    h_left.wait_recv()
    share[1].start()
    h_right.wait_recv()
    share[3].start()

    block = min(128, width)
    whole_blocks = vocab_here // 128
    tail[...] = jnp.zeros_like(tail)
    tail[pl.ds(0, vocab_here - whole_blocks * 128)] = head_v[pl.ds(whole_blocks * 128, vocab_here - whole_blocks * 128)]

    h_far.wait_recv()
    h_on.start()

    share[1].wait_recv()
    for piece, (at, size) in enumerate(PIECES):
        put(hold.at[0], at, 1, HALF + at, size)
        send_packed(snd2, 0, piece, hold[0, pl.ds(at, size)], ONE)
        packed_copy(0, 0, piece).start()
    share[3].wait_recv()
    for piece, (at, size) in enumerate(PIECES):
        put(hold.at[1], at, 3, at, size)
        send_packed(snd2, 1, piece, hold[1, pl.ds(at, size)], ONE)
        packed_copy(0, 1, piece).start()

    h_on.wait_recv()
    share[2].start()
    share[2].wait_recv()
    for piece, (at, size) in enumerate(PIECES):
        put(hold.at[0], at, 2, at, size)
        send_packed(snd1, 0, piece, hold[0, pl.ds(at, size)], ONE)
        packed_copy(1, 0, piece).start()
        put(hold.at[1], at, 2, HALF + at, size)
        send_packed(snd1, 1, piece, hold[1, pl.ds(at, size)], ONE)
        packed_copy(1, 1, piece).start()

    for at, size in PIECES:
        put(hold.at[0], at, 1, at, size)
        put(hold.at[1], at, 3, HALF + at, size)
    load_own.wait()
    for half in (0, HALF):
        for at, size in PIECES:
            put(logits, half + at, 0, half + at, size)

    def turn(j, carry):
        cols = pl.ds(pl.multiple_of(j * block, block), block)
        for i in range(whole_blocks):
            head_t[cols, pl.ds(i * 128, 128)] = head_v[pl.ds(i * 128, 128), cols].T
        head_t[cols, pl.ds(whole_blocks * 128, 128)] = tail[:, cols].T
        return carry

    lax.fori_loop(0, width // block, turn, 0)
    load_frozen.wait()
    frozen_f[pl.ds(1184, ROWS - 1184)] = jnp.zeros((ROWS - 1184, frozen_f.shape[1]), F32)
    frozen_f[pl.ds(0, vocab_here)] = frozen_v[...].astype(F32)

    def add_into(dst, at, piece, parts):
        quarter = PIECES[piece][1] // 4
        for k, part in enumerate(parts):
            rows = pl.ds(at + k * quarter, quarter)
            dst[rows] = dst[rows] + part

    for piece, (at, size) in enumerate(PIECES):
        for slot in (0, 1):
            packed_copy(1, slot, piece).wait_recv()
            add_into(hold.at[slot], at, piece, read_packed(rcv1, slot, piece, ONE))
            send_packed(snd3, slot, piece, hold[slot, pl.ds(at, size)], TWO)
            packed_copy(2, slot, piece).start()

    for slot in (0, 1):
        half = (HALF, 0)[slot]
        for piece, (at, size) in enumerate(PIECES):
            packed_copy(0, slot, piece).wait_recv()
            add_into(logits, half + at, piece, read_packed(rcv2, slot, piece, ONE))
    for piece, (at, size) in enumerate(PIECES):
        for slot in (0, 1):
            half = (0, HALF)[slot]
            packed_copy(2, slot, piece).wait_recv()
            add_into(logits, half + at, piece, read_packed(rcv3, slot, piece, TWO))

    edge = vocab_here // 8 * 8
    rows = edge + lax.broadcasted_iota(jnp.int32, (ROWS - edge, logits.shape[1]), 0)
    logits[pl.ds(edge, ROWS - edge)] = jnp.where(
        rows < vocab_here, logits[pl.ds(edge, ROWS - edge)], -1e30
    )

    step = ROWS // 4
    tops = [jnp.max(logits[pl.ds(k * step, step)], axis=0, keepdims=True) for k in range(4)]
    top = functools.reduce(jnp.maximum, tops)
    total = jnp.zeros_like(top)
    cross = jnp.zeros_like(top)
    for k in range(4):
        piece = pl.ds(k * step, step)
        shifted = jnp.exp(logits[piece] - top)
        total += jnp.sum(shifted, axis=0, keepdims=True)
        cross += jnp.sum(shifted * (logits[piece] - frozen_f[piece]), axis=0, keepdims=True)

    def exchange(top, total, cross, out, into, send, recv, to, count):
        out[0:1] = top
        out[1:2] = total
        out[2:3] = cross
        out[3:4] = cross

        def go(k, carry):
            remote(out, into.at[k], send.at[k], recv.at[k], to(k)).start()
            return carry

        def arrive(k, carry):
            remote(out, into.at[k], send.at[k], recv.at[k], to(k)).wait()
            return carry

        lax.fori_loop(1, count, go, 0)
        lax.fori_loop(1, count, arrive, 0)
        best = top
        for k in range(1, count):
            best = jnp.maximum(best, into[k, 0:1])
        scale = jnp.exp(top - best)
        all_total, all_cross = total * scale, cross * scale
        for k in range(1, count):
            scale = jnp.exp(into[k, 0:1] - best)
            all_total += into[k, 1:2] * scale
            all_cross += into[k, 2:3] * scale
        return best, all_total, all_cross

    top, total, cross = exchange(
        top, total, cross, st1, st1_in, s1_send, s1_recv, in_group, GROUP
    )
    top, total, cross = exchange(top, total, cross, st2, st2_in, s2_send, s2_recv, along_z, NZ)
    mean = cross / total
    out_div[...] = mean - top - jnp.log(total) + norms[...]

    for copy in counts:
        copy.wait()
    all_counts = cnt[...] + cnt_in[0] + cnt_in[1] + cnt_in[2]
    weight = cnt[...] / jnp.sum(all_counts, axis=1, keepdims=True)
    adv, ratio = advantages[...], ratios[...]
    active = jnp.where(adv >= 0.0, (ratio <= 1.0 + clip_eps).astype(F32), (ratio >= 1.0 - clip_eps).astype(F32))
    policy = jnp.where(active > 0.5, -adv * ratio, jnp.zeros_like(ratio))
    target = targets[...] - v * vocab_here
    target = jnp.where(target < vocab_here, target, -1)
    inverse = 1.0 / total
    hits = weight * policy

    def gradient_copy(slot, kind):
        device = ((right, left)[slot], v)
        half = (slot, 1 - slot, slot)[kind]
        rows = pl.ds(half * HALF, SENT[half])
        source = ((0, 0, 3), (0, 0, 1))[slot][kind]
        into = ((3, 3, 2), (1, 1, 2))[slot][kind]
        sem = slot * 3 + kind
        return remote(g.at[source, rows], g.at[into, rows], g_send.at[sem], g_recv.at[sem], device)

    for k in range(4):
        piece = pl.ds(k * step, step)
        value = logits[piece]
        chance = jnp.exp(value - top) * inverse
        rows = k * step + lax.broadcasted_iota(jnp.int32, value.shape, 0)
        grad = weight * (penalty * chance * (value - frozen_f[piece] - mean) - policy * chance)
        grad = jnp.where(rows == target, grad + hits, grad)
        g[0, piece] = grad.astype(BF16)
        if k == 1:
            gradient_copy(0, 0).start()
            gradient_copy(1, 1).start()
    gradient_copy(1, 0).start()
    gradient_copy(0, 1).start()

    chunk = width // 4
    units = chunk // 16

    def partial(sources):
        right_side = [g[r] for r in sources]
        right_side = right_side[0] if len(sources) == 1 else jnp.concatenate(right_side, axis=1)

        for i in range(4):
            value = jnp.dot(head_t[pl.ds(i * chunk, chunk)], right_side, preferred_element_type=F32)
            for j, r in enumerate(sources):
                prod[r, pl.ds(i * units, units)] = value[:, j * 128 : (j + 1) * 128].reshape(units, 2, 8, 128)
        for r in sources:
            pair(r).start()

    def pair(r):
        return remote(prod.at[r, :, 1 - core], prod_in.at[r], a_send.at[r], a_recv.at[r], sibling)

    def x_copy(r, k):
        sem = r * NX + k
        return remote(xs.at[r, k], xs_in.at[r, k], x_send.at[sem], x_recv.at[sem], along_x(k))

    def z_copy(r, k):
        sem = r * NZ + k
        return remote(
            zs.at[r, lax.rem(z + k, NZ)], zs_in.at[r, k], z_send.at[sem], z_recv.at[sem], along_z(k)
        )

    def to_x(r):
        pair(r).wait_recv()
        for k in range(NX):
            there = lax.rem(x + k, NX)
            value = mid_sum(r, there)
            if k == 0:
                mid[r] = value
            else:
                xs[r, k] = value.reshape(NZ * 8, 128).astype(BF16)
                x_copy(r, k).start()

    def mid_sum(r, there):
        return jnp.stack(
            [prod[r, zz * NX + there, core] + prod_in[r, zz * NX + there] for zz in range(NZ)]
        )

    def to_z(r):
        value = mid[r]
        for k in range(1, NX):
            x_copy(r, k).wait_recv()
            value = value + xs_in[r, k].astype(F32).reshape(NZ, 8, 128)
        zs[r] = value

        def go(k, carry):
            z_copy(r, k).start()
            return carry

        lax.fori_loop(1, NZ, go, 0)

    def finish(r):
        def arrive(k, carry):
            z_copy(r, k).wait_recv()
            return carry

        lax.fori_loop(1, NZ, arrive, 0)
        value = zs[r, z]
        for k in range(1, NZ):
            value = value + zs_in[r, k]
        tokens = lax.rem(me + r, 4) * 128
        total_h[:, pl.ds(pl.multiple_of(tokens, 128), 128)] = value

    head_rows = ((0, 304), (304, 304), (608, 304), (912, vocab_here - 912))

    def head_gradient(k):
        at, size = head_rows[k]
        rows = pl.ds(at, size)
        left_side = jnp.concatenate([g[r, rows] for r in range(4)], axis=1)
        tokens = hid[...].reshape(4 * hid.shape[1], width)
        head_o[rows] = jnp.dot(left_side, tokens, preferred_element_type=F32).astype(BF16)
        head_copy(k).start()

    def head_copy(k):
        at, size = head_rows[k]
        return pltpu.make_async_copy(head_o.at[pl.ds(at, size)], out_head.at[pl.ds(at, size)], o_sem.at[k])

    partial((0,))
    to_x(0)
    gradient_copy(0, 0).wait_recv()
    gradient_copy(0, 2).start()
    gradient_copy(1, 0).wait_recv()
    gradient_copy(1, 2).start()
    to_z(0)
    gradient_copy(0, 1).wait_recv()
    gradient_copy(1, 1).wait_recv()
    partial((1, 3))
    to_x(1)
    to_x(3)
    to_z(1)
    to_z(3)
    gradient_copy(0, 2).wait_recv()
    gradient_copy(1, 2).wait_recv()
    partial((2,))
    head_gradient(0)
    to_x(2)
    head_gradient(1)
    head_gradient(2)
    to_z(2)
    head_gradient(3)
    finish(0)
    finish(1)
    finish(3)
    finish(2)
    out_hidden[...] = total_h[...].astype(BF16)

    for copy in (h_right, h_left, h_far, h_on, share[1], share[2], share[3]):
        copy.wait_send()
    for stage in range(3):
        for slot in (0, 1):
            for piece in (0, 1):
                packed_copy(stage, slot, piece).wait_send()
    for slot in (0, 1):
        for kind in range(3):
            gradient_copy(slot, kind).wait_send()
    for r in range(4):
        pair(r).wait_send()
        for k in range(1, NX):
            x_copy(r, k).wait_send()

        def left_z(k, carry):
            z_copy(r, k).wait_send()
            return carry

        lax.fori_loop(1, NZ, left_z, 0)
    for k in range(4):
        head_copy(k).wait()


def local(devices, hidden, head, frozen, norms, advantages, ratios, targets, counted):
    tokens, depth = hidden.shape
    width = depth // 4
    vocab_here = head.shape[1]
    NZ = devices // (2 * NX)
    GROUP = 2 * NX
    units = width // 16
    packed = pltpu.VMEM((2, HALF // 4 * 3, tokens), jnp.int32)
    dma = pltpu.SemaphoreType.DMA
    row = [a.reshape(1, tokens) for a in (norms, advantages, ratios, targets, counted)]
    vmem = pl.BlockSpec(memory_space=pltpu.VMEM)
    anywhere = pl.BlockSpec(memory_space=pl.ANY)
    out = pl.pallas_call(
        functools.partial(kernel, devices),
        out_shape=(
            jax.ShapeDtypeStruct((width // devices, 4 * tokens), BF16),
            jax.ShapeDtypeStruct((vocab_here, width), BF16),
            jax.ShapeDtypeStruct((1, tokens), F32),
        ),
        in_specs=[anywhere] * 3 + [vmem] * 5,
        out_specs=(vmem, anywhere, vmem),
        scratch_shapes=[
            pltpu.VMEM((vocab_here, width), BF16),
            pltpu.VMEM((width, DEEP), BF16),
            pltpu.VMEM((128, width), BF16),
            pltpu.VMEM((vocab_here, tokens), BF16),
            pltpu.VMEM((ROWS, tokens), F32),
            pltpu.VMEM((4, tokens, width), BF16),
            pltpu.VMEM((tokens // 2, width), BF16),
            pltpu.VMEM((ROWS, tokens), F32),
            pltpu.VMEM((2, HALF, tokens), F32),
            packed, packed, packed, packed, packed, packed,
            pltpu.VMEM((1, tokens), F32),
            pltpu.VMEM((3, 1, tokens), F32),
            pltpu.VMEM((4, tokens), F32),
            pltpu.VMEM((GROUP, 4, tokens), F32),
            pltpu.VMEM((4, tokens), F32),
            pltpu.VMEM((NZ, 4, tokens), F32),
            pltpu.VMEM((4, DEEP, tokens), BF16),
            pltpu.VMEM((4, units, 2, 8, tokens), F32),
            pltpu.VMEM((4, units, 8, tokens), F32),
            pltpu.VMEM((4, NZ, 8, tokens), F32),
            pltpu.VMEM((4, NX, NZ * 8, tokens), BF16),
            pltpu.VMEM((4, NX, NZ * 8, tokens), BF16),
            pltpu.VMEM((4, NZ, 8, tokens), F32),
            pltpu.VMEM((4, NZ, 8, tokens), F32),
            pltpu.VMEM((8, 4 * tokens), F32),
            pltpu.VMEM((vocab_here, width), BF16),
            dma((3,)),
            dma((4,)), dma((4,)),
            dma((4,)), dma((4,)),
            dma((12,)), dma((12,)),
            dma((3,)), dma((3,)),
            dma((GROUP,)), dma((GROUP,)),
            dma((NZ,)), dma((NZ,)),
            dma((6,)), dma((6,)),
            dma((4,)), dma((4,)),
            dma((4 * NX,)), dma((4 * NX,)),
            dma((4 * NZ,)), dma((4 * NZ,)),
            dma((4,)),
        ],
        compiler_params=pltpu.CompilerParams(
            collective_id=0, has_side_effects=True, vmem_limit_bytes=48 * 1024 * 1024
        ),
    )(hidden, head.T, frozen.T, *row)
    return out[0].T, out[1].T, out[2].reshape(tokens)


def solution(mesh):
    return jax.shard_map(
        functools.partial(local, mesh.shape["vocab"]),
        mesh=mesh,
        in_specs=(
            P("dp", None),
            P("dp", "vocab"),
            P("dp", "vocab"),
            P("dp"),
            P("dp"),
            P("dp"),
            P("dp"),
            P("dp"),
        ),
        out_specs=(P(None, ("dp", "vocab")), P("dp", "vocab"), P("dp")),
        check_vma=False,
    )
```

```python
import functools

import jax
import jax.numpy as jnp
from jax import lax
from jax.experimental import pallas as pl
from jax.experimental.pallas import tpu as pltpu
from jax.sharding import PartitionSpec as P

clip_eps = 0.2
penalty = 0.1

NX = 4
HALF = 608
PIECES = ((0, 320), (320, 288))
SENT = (608, 592)
ROWS = 2 * HALF
DEEP = 1280
ONE = 512.0
TWO = 256.0
MESH = pl.DeviceIdType.MESH
F32 = jnp.float32
BF16 = jnp.bfloat16


def pack(values, scale):
    top = 8388607.0
    whole = jnp.clip(jnp.floor(values * scale + 0.5), -top, top).astype(jnp.int32)
    quarter = values.shape[0] // 4
    a, b, c, d = (whole[k * quarter : (k + 1) * quarter] for k in range(4))
    low = 0xFFFFFF
    return (
        (a & low) | (d << 24),
        (b & low) | ((d >> 8) << 24),
        (c & low) | ((d >> 16) << 24),
    )


def unpack(u, v, w, scale):
    parts = [(word << 8) >> 8 for word in (u, v, w)]
    parts.append(((u >> 24) & 0xFF) | (((v >> 24) & 0xFF) << 8) | ((w >> 24) << 16))
    back = 1.0 / scale
    return [part.astype(F32) * back for part in parts]


def kernel(
    devices,
    hidden, head, frozen, norms_h, advantages_h, ratios_h, targets_h, counted_h,
    out_hidden, out_head, out_div,
    norms, advantages, ratios, targets, counted, head_v, head_t, tail, frozen_v, frozen_f, hid, via, logits, hold,
    snd2, snd1, snd3, rcv2, rcv1, rcv3,
    cnt, cnt_in, st1, st1_in, st2, st2_in,
    g, prod, prod_in, mid, xs, xs_in, zs, zs_in, total_h,
    load_sem, h_send, h_recv, sh_send, sh_recv, r_send, r_recv,
    c_send, c_recv, s1_send, s1_recv, s2_send, s2_recv,
    g_send, g_recv, a_send, a_recv, x_send, x_recv, z_send, z_recv, f_sem, hello,
):
    NZ = devices // (2 * NX)
    GROUP = 2 * NX
    width = hid.shape[2]
    vocab_here = head.shape[0]
    me = lax.axis_index("dp")
    v = lax.axis_index("vocab")
    core = lax.rem(v, 2)
    x = lax.rem(v // 2, NX)
    z = v // GROUP
    xc = lax.rem(v, GROUP)
    right, far, left = (lax.rem(me + k, 4) for k in (1, 2, 3))
    sibling = (me, v + 1 - 2 * core)

    def in_group(k):
        return (me, z * GROUP + lax.rem(xc + k, GROUP))

    def along_x(k):
        return (me, z * GROUP + lax.rem(x + k, NX) * 2 + core)

    def along_z(k):
        return (me, lax.rem(z + k, NZ) * GROUP + xc)

    def remote(src, dst, send, recv, device):
        return pltpu.make_async_remote_copy(
            src_ref=src, dst_ref=dst, send_sem=send, recv_sem=recv,
            device_id=device, device_id_type=MESH,
        )

    def lanes(block):
        return pl.ds(pl.multiple_of(block * width, width), width)

    half_tok = hid.shape[1] // 2
    mine = pl.ds(pl.multiple_of(core * half_tok, half_tok), half_tok)

    load_head = pltpu.make_async_copy(head, head_v, load_sem.at[0])
    load_own = pltpu.make_async_copy(hidden.at[:, lanes(me)], hid.at[0], load_sem.at[1])
    load_frozen = pltpu.make_async_copy(frozen, frozen_v, load_sem.at[2])
    load_rows = [
        pltpu.make_async_copy(src, dst, load_sem.at[3 + k])
        for k, (src, dst) in enumerate((
            (counted_h, counted), (norms_h, norms), (advantages_h, advantages),
            (ratios_h, ratios), (targets_h, targets),
        ))
    ]
    load_rows[0].start()
    load_head.start()
    load_own.start()
    load_frozen.start()
    for copy in load_rows[1:]:
        copy.start()
    barrier = pltpu.get_barrier_semaphore()

    near_y = [(lax.rem(me + k, 4), v) for k in (1, 3)]
    near_x = [along_x(k) for k in (1, NX - 1)]

    def near_z(k):
        return [along_z(k), along_z(NZ - k)]

    nearest = [sibling, *near_y, *near_x, *near_z(1)]
    for device in nearest:
        pl.semaphore_signal(barrier, inc=1, device_id=device, device_id_type=MESH)
    rounds = (near_y + near_x + near_z(1), near_x + near_z(2), near_z(4))

    def tell(n):
        for device in rounds[n]:
            pl.semaphore_signal(hello.at[n], inc=1, device_id=device, device_id_type=MESH)

    def heard(n):
        pl.semaphore_wait(hello.at[n], len(rounds[n]))

    load_rows[0].wait()
    cnt[...] = counted[...].astype(F32)
    pl.semaphore_wait(barrier, len(nearest))

    onward = (lax.rem(me + 1 + 2 * core, 4), v)
    h_right = remote(hidden.at[mine, lanes(right)], hid.at[3, mine], h_send.at[0], h_recv.at[0], (right, v))
    h_left = remote(hidden.at[mine, lanes(left)], hid.at[1, mine], h_send.at[1], h_recv.at[1], (left, v))
    h_far = remote(hidden.at[mine, lanes(far)], via, h_send.at[2], h_recv.at[2], onward)
    h_on = remote(via, hid.at[2, mine], h_send.at[3], h_recv.at[3], onward)
    h_far.start()
    h_right.start()
    h_left.start()
    counts = [
        remote(cnt, cnt_in.at[k - 1], c_send.at[k - 1], c_recv.at[k - 1], (lax.rem(me + k, 4), v))
        for k in (1, 2, 3)
    ]
    tell(0)
    share = {
        r: remote(hid.at[r, mine], hid.at[r, mine], sh_send.at[r], sh_recv.at[r], sibling)
        for r in (1, 2, 3)
    }

    for r in range(4):
        g[r, pl.ds(1184, DEEP - 1184)] = jnp.zeros((DEEP - 1184, g.shape[2]), BF16)
    tail[...] = jnp.zeros_like(tail)
    load_head.wait()

    def product(r, start, size):
        valid = min(size, vocab_here - start)
        rows = head_v[pl.ds(start, valid)]
        return valid, lax.dot_general(
            rows, hid[r], (((1,), (1,)), ((), ())), preferred_element_type=F32
        )

    def put(dst, at, r, start, size):
        valid, value = product(r, start, size)
        if valid < size:
            floor = valid // 8 * 8
            dst[pl.ds(at + floor, size - floor)] = jnp.zeros((size - floor, value.shape[1]), F32)
        dst[pl.ds(at, valid)] = value

    def send_packed(buffer, slot, piece, values, scale):
        at, size = PIECES[piece]
        quarter, at = size // 4, at // 4 * 3
        for k, words in enumerate(pack(values, scale)):
            buffer[slot, pl.ds(at + k * quarter, quarter)] = words

    def read_packed(buffer, slot, piece, scale):
        at, size = PIECES[piece]
        quarter, at = size // 4, at // 4 * 3
        return unpack(*(buffer[slot, pl.ds(at + k * quarter, quarter)] for k in range(3)), scale)

    def packed_copy(step, slot, piece):
        snd, rcv = ((snd2, rcv2), (snd1, rcv1), (snd3, rcv3))[step]
        at, size = PIECES[piece]
        rows = pl.ds(at // 4 * 3, size // 4 * 3)
        sem = (step * 2 + slot) * 2 + piece
        return remote(
            snd.at[slot, rows], rcv.at[slot, rows], r_send.at[sem], r_recv.at[sem],
            ((right, left)[slot], v),
        )

    h_far.wait_recv()
    h_on.start()
    h_left.wait_recv()
    share[1].start()
    h_right.wait_recv()
    share[3].start()

    heard(0)
    tell(1)
    for copy in counts:
        copy.start()

    block = min(128, width)
    whole_blocks = vocab_here // 128
    tail[pl.ds(0, vocab_here - whole_blocks * 128)] = head_v[pl.ds(whole_blocks * 128, vocab_here - whole_blocks * 128)]

    share[1].wait_recv()
    for piece, (at, size) in enumerate(PIECES):
        put(hold.at[0], at, 1, HALF + at, size)
        send_packed(snd2, 0, piece, hold[0, pl.ds(at, size)], ONE)
        packed_copy(0, 0, piece).start()
    share[3].wait_recv()
    for piece, (at, size) in enumerate(PIECES):
        put(hold.at[1], at, 3, at, size)
        send_packed(snd2, 1, piece, hold[1, pl.ds(at, size)], ONE)
        packed_copy(0, 1, piece).start()

    heard(1)
    tell(2)

    h_on.wait_recv()
    share[2].start()
    share[2].wait_recv()
    for piece, (at, size) in enumerate(PIECES):
        put(hold.at[0], at, 2, at, size)
        send_packed(snd1, 0, piece, hold[0, pl.ds(at, size)], ONE)
        packed_copy(1, 0, piece).start()
        put(hold.at[1], at, 2, HALF + at, size)
        send_packed(snd1, 1, piece, hold[1, pl.ds(at, size)], ONE)
        packed_copy(1, 1, piece).start()

    for at, size in PIECES:
        put(hold.at[0], at, 1, at, size)
        put(hold.at[1], at, 3, HALF + at, size)
    load_own.wait()
    for half in (0, HALF):
        for at, size in PIECES:
            put(logits, half + at, 0, half + at, size)

    def turn(j, carry):
        cols = pl.ds(pl.multiple_of(j * block, block), block)
        for i in range(whole_blocks):
            head_t[cols, pl.ds(i * 128, 128)] = head_v[pl.ds(i * 128, 128), cols].T
        head_t[cols, pl.ds(whole_blocks * 128, 128)] = tail[:, cols].T
        return carry

    lax.fori_loop(0, width // block, turn, 0)
    load_frozen.wait()
    for copy in load_rows[1:]:
        copy.wait()
    frozen_f[pl.ds(1184, ROWS - 1184)] = jnp.zeros((ROWS - 1184, frozen_f.shape[1]), F32)
    frozen_f[pl.ds(0, vocab_here)] = frozen_v[...].astype(F32)

    def add_into(dst, at, piece, parts):
        quarter = PIECES[piece][1] // 4
        for k, part in enumerate(parts):
            rows = pl.ds(at + k * quarter, quarter)
            dst[rows] = dst[rows] + part

    for piece, (at, size) in enumerate(PIECES):
        for slot in (0, 1):
            packed_copy(1, slot, piece).wait_recv()
            add_into(hold.at[slot], at, piece, read_packed(rcv1, slot, piece, ONE))
            send_packed(snd3, slot, piece, hold[slot, pl.ds(at, size)], TWO)
            packed_copy(2, slot, piece).start()

    heard(2)

    for slot in (0, 1):
        half = (HALF, 0)[slot]
        for piece, (at, size) in enumerate(PIECES):
            packed_copy(0, slot, piece).wait_recv()
            add_into(logits, half + at, piece, read_packed(rcv2, slot, piece, ONE))
    for piece, (at, size) in enumerate(PIECES):
        for slot in (0, 1):
            half = (0, HALF)[slot]
            packed_copy(2, slot, piece).wait_recv()
            add_into(logits, half + at, piece, read_packed(rcv3, slot, piece, TWO))

    edge = vocab_here // 8 * 8
    rows = edge + lax.broadcasted_iota(jnp.int32, (ROWS - edge, logits.shape[1]), 0)
    logits[pl.ds(edge, ROWS - edge)] = jnp.where(
        rows < vocab_here, logits[pl.ds(edge, ROWS - edge)], -1e30
    )

    step = ROWS // 4
    tops = [jnp.max(logits[pl.ds(k * step, step)], axis=0, keepdims=True) for k in range(4)]
    top = functools.reduce(jnp.maximum, tops)
    total = jnp.zeros_like(top)
    cross = jnp.zeros_like(top)
    for k in range(4):
        piece = pl.ds(k * step, step)
        shifted = jnp.exp(logits[piece] - top)
        total += jnp.sum(shifted, axis=0, keepdims=True)
        cross += jnp.sum(shifted * (logits[piece] - frozen_f[piece]), axis=0, keepdims=True)

    def exchange(top, total, cross, out, into, send, recv, to, count):
        out[0:1] = top
        out[1:2] = total
        out[2:3] = cross
        out[3:4] = cross

        def go(k, carry):
            remote(out, into.at[k], send.at[k], recv.at[k], to(k)).start()
            return carry

        def arrive(k, carry):
            remote(out, into.at[k], send.at[k], recv.at[k], to(k)).wait()
            return carry

        lax.fori_loop(1, count, go, 0)
        lax.fori_loop(1, count, arrive, 0)
        best = top
        for k in range(1, count):
            best = jnp.maximum(best, into[k, 0:1])
        scale = jnp.exp(top - best)
        all_total, all_cross = total * scale, cross * scale
        for k in range(1, count):
            scale = jnp.exp(into[k, 0:1] - best)
            all_total += into[k, 1:2] * scale
            all_cross += into[k, 2:3] * scale
        return best, all_total, all_cross

    top, total, cross = exchange(
        top, total, cross, st1, st1_in, s1_send, s1_recv, in_group, GROUP
    )
    top, total, cross = exchange(top, total, cross, st2, st2_in, s2_send, s2_recv, along_z, NZ)
    mean = cross / total
    out_div[...] = mean - top - jnp.log(total) + norms[...]

    for copy in counts:
        copy.wait()
    all_counts = cnt[...] + cnt_in[0] + cnt_in[1] + cnt_in[2]
    weight = cnt[...] / jnp.sum(all_counts, axis=1, keepdims=True)
    adv, ratio = advantages[...], ratios[...]
    open_ = jnp.where(adv >= 0.0, (ratio <= 1.0 + clip_eps).astype(F32), (ratio >= 1.0 - clip_eps).astype(F32))
    policy = jnp.where(open_ > 0.5, -adv * ratio, jnp.zeros_like(ratio))
    target = targets[...] - v * vocab_here
    target = jnp.where(target < vocab_here, target, -1)
    inverse = 1.0 / total
    hits = weight * policy

    def gradient_copy(slot, kind):
        device = ((right, left)[slot], v)
        half = (slot, 1 - slot, slot)[kind]
        rows = pl.ds(half * HALF, SENT[half])
        source = ((0, 0, 3), (0, 0, 1))[slot][kind]
        into = ((3, 3, 2), (1, 1, 2))[slot][kind]
        sem = slot * 3 + kind
        return remote(g.at[source, rows], g.at[into, rows], g_send.at[sem], g_recv.at[sem], device)

    for k in range(4):
        piece = pl.ds(k * step, step)
        value = logits[piece]
        chance = jnp.exp(value - top) * inverse
        rows = k * step + lax.broadcasted_iota(jnp.int32, value.shape, 0)
        grad = weight * (penalty * chance * (value - frozen_f[piece] - mean) - policy * chance)
        grad = jnp.where(rows == target, grad + hits, grad)
        g[0, piece] = grad.astype(BF16)
        if k == 1:
            gradient_copy(0, 0).start()
            gradient_copy(1, 1).start()
    gradient_copy(1, 0).start()
    gradient_copy(0, 1).start()

    chunk = width // 4
    active = lax.rem(z, 2) == core
    sender = lax.rem(z, 2) != core

    def partial(sources):
        right_side = [g[r] for r in sources]
        right_side = right_side[0] if len(sources) == 1 else jnp.concatenate(right_side, axis=1)
        deep = NZ // 8
        for i in range(4):
            value = jnp.dot(head_t[pl.ds(i * chunk, chunk)], right_side, preferred_element_type=F32)
            for j, r in enumerate(sources):
                prod[r, pl.ds(i * deep, deep)] = value[:, j * 128 : (j + 1) * 128].reshape(
                    deep, 2, NX, 16, 128
                )
        for r in sources:
            pair(r).start()

    def pair(r):
        return remote(prod.at[r, :, 1 - core], prod_in.at[r], a_send.at[r], a_recv.at[r], sibling)

    def x_copy(r, k):
        sem = r * NX + k
        return remote(xs.at[r, k], xs_in.at[r, k], x_send.at[sem], x_recv.at[sem], along_x(k))

    def z_copy(r, k):
        m = lax.rem(z // 2 + k, NZ // 2)
        there = 2 * m + core
        slot = lax.rem(z - there + NZ, NZ)
        return remote(
            zs.at[r, m], zs_in.at[r, slot], z_send.at[r * NZ + k], z_recv.at[r * NZ + slot],
            (me, there * GROUP + xc),
        )

    def to_x(r):
        pair(r).wait_recv()
        for k in (*range(1, NX), 0):
            there = lax.rem(x + k, NX)
            value = prod[r, :, core, there] + prod_in[r, :, there]
            if k == 0:
                mid[r] = value
            else:
                xs[r, k] = value.reshape(NZ * 8, 128).astype(BF16)
                x_copy(r, k).start()

    def to_z(r):
        value = mid[r]
        for k in range(1, NX):
            x_copy(r, k).wait_recv()
            value = value + xs_in[r, k].astype(F32).reshape(NZ // 2, 16, 128)
        mid[r] = value
        zs[r] = value.astype(BF16)

        def go(k, carry):
            z_copy(r, k).start()
            return carry

        lax.fori_loop(1, NZ // 2, go, 0)

        @pl.when(sender)
        def _():
            z_copy(r, 0).start()

    def finish(r):
        def arrive(k, carry):
            remote(
                zs.at[r, 0], zs_in.at[r, k], z_send.at[r * NZ], z_recv.at[r * NZ + k],
                (me, lax.rem(z + k, NZ) * GROUP + xc),
            ).wait_recv()
            return carry

        lax.fori_loop(1, NZ, arrive, 0)
        value = mid[r, z // 2]
        for k in range(1, NZ):
            value = value + zs_in[r, k].astype(F32)
        tokens = pl.ds(pl.multiple_of(lax.rem(me + r, 4) * 128, 128), 128)
        total_h[0, :, tokens] = value[:8]
        total_h[1, :, tokens] = value[8:]

    last = remote(
        total_h.at[1 - core], total_h.at[1 - core], f_sem.at[0], f_sem.at[1], sibling
    )

    head_rows = ((0, 304), (304, 304), (608, 304), (912, vocab_here - 912))

    def head_gradient(k):
        at, size = head_rows[k]
        rows = pl.ds(at, size)
        left_side = jnp.concatenate([g[r, rows] for r in range(4)], axis=1)
        tokens = hid[...].reshape(4 * hid.shape[1], width)
        out_head[rows] = jnp.dot(left_side, tokens, preferred_element_type=F32).astype(BF16)

    partial((0,))
    gradient_copy(0, 0).wait_recv()
    gradient_copy(0, 2).start()
    gradient_copy(1, 0).wait_recv()
    gradient_copy(1, 2).start()
    to_x(0)
    to_z(0)
    gradient_copy(0, 1).wait_recv()
    gradient_copy(1, 1).wait_recv()
    partial((1, 3))
    to_x(1)
    to_x(3)
    gradient_copy(0, 2).wait_recv()
    gradient_copy(1, 2).wait_recv()
    partial((2,))
    head_gradient(0)
    to_x(2)
    to_z(1)
    to_z(3)
    head_gradient(1)
    head_gradient(2)
    to_z(2)
    head_gradient(3)

    @pl.when(active)
    def _():
        for r in (0, 1, 3, 2):
            finish(r)
        last.start()
        last.wait_send()

    @pl.when(sender)
    def _():
        last.wait_recv()

    out_hidden[...] = total_h[core].astype(BF16)

    for copy in (h_right, h_left, h_far, h_on, share[1], share[2], share[3]):
        copy.wait_send()
    for stage in range(3):
        for slot in (0, 1):
            for piece in (0, 1):
                packed_copy(stage, slot, piece).wait_send()
    for slot in (0, 1):
        for kind in range(3):
            gradient_copy(slot, kind).wait_send()
    for r in range(4):
        pair(r).wait_send()
        for k in range(1, NX):
            x_copy(r, k).wait_send()

        def left_z(k, carry):
            z_copy(r, k).wait_send()
            return carry

        lax.fori_loop(1, NZ // 2, left_z, 0)

        @pl.when(sender)
        def _():
            z_copy(r, 0).wait_send()


def local(devices, hidden, head, frozen, norms, advantages, ratios, targets, counted):
    tokens, depth = hidden.shape
    width = depth // 4
    vocab_here = head.shape[1]
    NZ = devices // (2 * NX)
    GROUP = 2 * NX
    packed = pltpu.VMEM((2, HALF // 4 * 3, tokens), jnp.int32)
    dma = pltpu.SemaphoreType.DMA
    row = [a.reshape(1, tokens) for a in (norms, advantages, ratios, targets, counted)]
    vmem = pl.BlockSpec(memory_space=pltpu.VMEM)
    out = pl.pallas_call(
        functools.partial(kernel, devices),
        out_shape=(
            jax.ShapeDtypeStruct((width // devices, 4 * tokens), BF16),
            jax.ShapeDtypeStruct((vocab_here, width), BF16),
            jax.ShapeDtypeStruct((1, tokens), F32),
        ),
        in_specs=[pl.BlockSpec(memory_space=pltpu.HBM)] * 8,
        out_specs=(vmem, vmem, vmem),
        scratch_shapes=[
            pltpu.VMEM((1, tokens), F32),
            pltpu.VMEM((1, tokens), F32),
            pltpu.VMEM((1, tokens), F32),
            pltpu.VMEM((1, tokens), jnp.int32),
            pltpu.VMEM((1, tokens), jnp.int32),
            pltpu.VMEM((vocab_here, width), BF16),
            pltpu.VMEM((width, DEEP), BF16),
            pltpu.VMEM((128, width), BF16),
            pltpu.VMEM((vocab_here, tokens), BF16),
            pltpu.VMEM((ROWS, tokens), F32),
            pltpu.VMEM((4, tokens, width), BF16),
            pltpu.VMEM((tokens // 2, width), BF16),
            pltpu.VMEM((ROWS, tokens), F32),
            pltpu.VMEM((2, HALF, tokens), F32),
            packed, packed, packed, packed, packed, packed,
            pltpu.VMEM((1, tokens), F32),
            pltpu.VMEM((3, 1, tokens), F32),
            pltpu.VMEM((4, tokens), F32),
            pltpu.VMEM((GROUP, 4, tokens), F32),
            pltpu.VMEM((4, tokens), F32),
            pltpu.VMEM((NZ, 4, tokens), F32),
            pltpu.VMEM((4, DEEP, tokens), BF16),
            pltpu.VMEM((4, NZ // 2, 2, NX, 16, tokens), F32),
            pltpu.VMEM((4, NZ // 2, NX, 16, tokens), F32),
            pltpu.VMEM((4, NZ // 2, 16, tokens), F32),
            pltpu.VMEM((4, NX, NZ * 8, tokens), BF16),
            pltpu.VMEM((4, NX, NZ * 8, tokens), BF16),
            pltpu.VMEM((4, NZ // 2, 16, tokens), BF16),
            pltpu.VMEM((4, NZ, 16, tokens), BF16),
            pltpu.VMEM((2, 8, 4 * tokens), F32),
            dma((8,)),
            dma((4,)), dma((4,)),
            dma((4,)), dma((4,)),
            dma((12,)), dma((12,)),
            dma((3,)), dma((3,)),
            dma((GROUP,)), dma((GROUP,)),
            dma((NZ,)), dma((NZ,)),
            dma((6,)), dma((6,)),
            dma((4,)), dma((4,)),
            dma((4 * NX,)), dma((4 * NX,)),
            dma((4 * NZ,)), dma((4 * NZ,)),
            dma((2,)),
            pltpu.SemaphoreType.REGULAR((3,)),
        ],
        compiler_params=pltpu.CompilerParams(
            collective_id=0, has_side_effects=True, vmem_limit_bytes=48 * 1024 * 1024
        ),
    )(*(pltpu.with_memory_space_constraint(a, pltpu.HBM) for a in (hidden, head.T, frozen.T, *row)))
    return out[0].T, out[1].T, out[2].reshape(tokens)


def solution(mesh):
    return jax.shard_map(
        functools.partial(local, mesh.shape["vocab"]),
        mesh=mesh,
        in_specs=(
            P("dp", None),
            P("dp", "vocab"),
            P("dp", "vocab"),
            P("dp"),
            P("dp"),
            P("dp"),
            P("dp"),
            P("dp"),
        ),
        out_specs=(P(None, ("dp", "vocab")), P("dp", "vocab"), P("dp")),
        check_vma=False,
    )
```

```python
import functools

import jax
import jax.numpy as jnp
from jax import lax
from jax.experimental import pallas as pl
from jax.experimental.pallas import tpu as pltpu
from jax.sharding import PartitionSpec as P

clip_eps = 0.2
penalty = 0.1

NX = 4
HALF = 608
PIECES = ((0, 320), (320, 288))
EARLY = 320
LATE = (288, 272)
ROWS = 2 * HALF
DEEP = 1280
ONE = 512.0
TWO = 256.0
MESH = pl.DeviceIdType.MESH
F32 = jnp.float32
BF16 = jnp.bfloat16


def pack(values, scale):
    top = 8388607.0
    whole = jnp.clip(jnp.floor(values * scale + 0.5), -top, top).astype(jnp.int32)
    quarter = values.shape[0] // 4
    a, b, c, d = (whole[k * quarter : (k + 1) * quarter] for k in range(4))
    low = 0xFFFFFF
    return (
        (a & low) | (d << 24),
        (b & low) | ((d >> 8) << 24),
        (c & low) | ((d >> 16) << 24),
    )


def unpack(u, v, w, scale):
    parts = [(word << 8) >> 8 for word in (u, v, w)]
    parts.append(((u >> 24) & 0xFF) | (((v >> 24) & 0xFF) << 8) | ((w >> 24) << 16))
    back = 1.0 / scale
    return [part.astype(F32) * back for part in parts]


def kernel(
    devices,
    hidden, head, frozen, norms_h, advantages_h, ratios_h, targets_h, counted_h,
    out_hidden, out_head, out_div,
    norms, advantages, ratios, targets, counted, head_v, head_t, tail, frozen_v, frozen_f, hid, via, logits, hold,
    snd2, snd1, snd3, rcv2, rcv1, rcv3,
    cnt, cnt_in, st1, st1_in, st2, st2_in,
    eu, terms, terms_in, g, prod, prod_in, mid, xs, xs_in, zs, zs_in, total_h,
    load_sem, h_send, h_recv, sh_send, sh_recv, r_send, r_recv,
    c_send, c_recv, s1_send, s1_recv, s2_send, s2_recv,
    e_send, e_recv, t_send, t_recv, g_send, g_recv, a_send, a_recv, x_send, x_recv, z_send, z_recv, f_sem, hello,
):
    NZ = devices // (2 * NX)
    GROUP = 2 * NX
    width = hid.shape[2]
    vocab_here = head.shape[0]
    me = lax.axis_index("dp")
    v = lax.axis_index("vocab")
    core = lax.rem(v, 2)
    x = lax.rem(v // 2, NX)
    z = v // GROUP
    xc = lax.rem(v, GROUP)
    right, far, left = (lax.rem(me + k, 4) for k in (1, 2, 3))
    sibling = (me, v + 1 - 2 * core)

    def in_group(k):
        return (me, z * GROUP + lax.rem(xc + k, GROUP))

    def along_x(k):
        return (me, z * GROUP + lax.rem(x + k, NX) * 2 + core)

    def along_z(k):
        return (me, lax.rem(z + k, NZ) * GROUP + xc)

    def remote(src, dst, send, recv, device):
        return pltpu.make_async_remote_copy(
            src_ref=src, dst_ref=dst, send_sem=send, recv_sem=recv,
            device_id=device, device_id_type=MESH,
        )

    def lanes(block):
        return pl.ds(pl.multiple_of(block * width, width), width)

    half_tok = hid.shape[1] // 2
    mine = pl.ds(pl.multiple_of(core * half_tok, half_tok), half_tok)

    load_head = pltpu.make_async_copy(head, head_v, load_sem.at[0])
    load_own = pltpu.make_async_copy(hidden.at[:, lanes(me)], hid.at[0], load_sem.at[1])
    load_frozen = pltpu.make_async_copy(frozen, frozen_v, load_sem.at[2])
    load_rows = [
        pltpu.make_async_copy(src, dst, load_sem.at[3 + k])
        for k, (src, dst) in enumerate((
            (counted_h, counted), (norms_h, norms), (advantages_h, advantages),
            (ratios_h, ratios), (targets_h, targets),
        ))
    ]
    load_rows[0].start()
    load_head.start()
    load_own.start()
    load_frozen.start()
    for copy in load_rows[1:]:
        copy.start()
    barrier = pltpu.get_barrier_semaphore()

    near_y = [(lax.rem(me + k, 4), v) for k in (1, 3)]
    near_x = [along_x(k) for k in (1, NX - 1)] if NX > 1 else []

    def near_z(k):
        return [along_z(k), along_z(NZ - k)]

    nearest = [sibling, *near_y, *near_x, *near_z(1)]
    for device in nearest:
        pl.semaphore_signal(barrier, inc=1, device_id=device, device_id_type=MESH)
    rounds = (near_y + near_x + near_z(1), near_x + near_z(2), near_z(4))

    def tell(n):
        for device in rounds[n]:
            pl.semaphore_signal(hello.at[n], inc=1, device_id=device, device_id_type=MESH)

    def heard(n):
        pl.semaphore_wait(hello.at[n], len(rounds[n]))

    load_rows[0].wait()
    cnt[...] = counted[...].astype(F32)
    pl.semaphore_wait(barrier, len(nearest))

    onward = (lax.rem(me + 1 + 2 * core, 4), v)
    h_right = remote(hidden.at[mine, lanes(right)], hid.at[3, mine], h_send.at[0], h_recv.at[0], (right, v))
    h_left = remote(hidden.at[mine, lanes(left)], hid.at[1, mine], h_send.at[1], h_recv.at[1], (left, v))
    h_far = remote(hidden.at[mine, lanes(far)], via, h_send.at[2], h_recv.at[2], onward)
    h_on = remote(via, hid.at[2, mine], h_send.at[3], h_recv.at[3], onward)
    h_right.start()
    h_left.start()
    h_far.start()
    counts = [
        remote(cnt, cnt_in.at[k - 1], c_send.at[k - 1], c_recv.at[k - 1], (lax.rem(me + k, 4), v))
        for k in (1, 2, 3)
    ]
    tell(0)
    share = {
        r: remote(hid.at[r, mine], hid.at[r, mine], sh_send.at[r], sh_recv.at[r], sibling)
        for r in (1, 2, 3)
    }

    for r in range(4):
        g[r, pl.ds(1184, DEEP - 1184)] = jnp.zeros((DEEP - 1184, g.shape[2]), BF16)
    tail[...] = jnp.zeros_like(tail)
    load_head.wait()

    def product(r, start, size):
        valid = min(size, vocab_here - start)
        rows = head_v[pl.ds(start, valid)]
        return valid, lax.dot_general(
            rows, hid[r], (((1,), (1,)), ((), ())), preferred_element_type=F32
        )

    def put(dst, at, r, start, size):
        valid, value = product(r, start, size)
        if valid < size:
            floor = valid // 8 * 8
            dst[pl.ds(at + floor, size - floor)] = jnp.zeros((size - floor, value.shape[1]), F32)
        dst[pl.ds(at, valid)] = value

    def send_packed(buffer, slot, piece, values, scale):
        at, size = PIECES[piece]
        quarter, at = size // 4, at // 4 * 3
        for k, words in enumerate(pack(values, scale)):
            buffer[slot, pl.ds(at + k * quarter, quarter)] = words

    def read_packed(buffer, slot, piece, scale):
        at, size = PIECES[piece]
        quarter, at = size // 4, at // 4 * 3
        return unpack(*(buffer[slot, pl.ds(at + k * quarter, quarter)] for k in range(3)), scale)

    def packed_copy(step, slot, piece):
        snd, rcv = ((snd2, rcv2), (snd1, rcv1), (snd3, rcv3))[step]
        at, size = PIECES[piece]
        rows = pl.ds(at // 4 * 3, size // 4 * 3)
        sem = (step * 2 + slot) * 2 + piece
        return remote(
            snd.at[slot, rows], rcv.at[slot, rows], r_send.at[sem], r_recv.at[sem],
            ((right, left)[slot], v),
        )

    h_left.wait_recv()
    share[1].start()
    h_right.wait_recv()
    share[3].start()
    h_far.wait_recv()
    h_on.start()

    heard(0)
    tell(1)
    for copy in counts:
        copy.start()

    block = min(128, width)
    whole_blocks = vocab_here // 128
    tail[pl.ds(0, vocab_here - whole_blocks * 128)] = head_v[pl.ds(whole_blocks * 128, vocab_here - whole_blocks * 128)]

    share[1].wait_recv()
    for piece, (at, size) in enumerate(PIECES):
        put(hold.at[0], at, 1, HALF + at, size)
        send_packed(snd2, 0, piece, hold[0, pl.ds(at, size)], ONE)
        packed_copy(0, 0, piece).start()
    share[3].wait_recv()
    for piece, (at, size) in enumerate(PIECES):
        put(hold.at[1], at, 3, at, size)
        send_packed(snd2, 1, piece, hold[1, pl.ds(at, size)], ONE)
        packed_copy(0, 1, piece).start()

    heard(1)
    tell(2)

    h_on.wait_recv()
    share[2].start()
    share[2].wait_recv()
    for piece, (at, size) in enumerate(PIECES):
        put(hold.at[0], at, 2, at, size)
        send_packed(snd1, 0, piece, hold[0, pl.ds(at, size)], ONE)
        packed_copy(1, 0, piece).start()
        put(hold.at[1], at, 2, HALF + at, size)
        send_packed(snd1, 1, piece, hold[1, pl.ds(at, size)], ONE)
        packed_copy(1, 1, piece).start()

    for at, size in PIECES:
        put(hold.at[0], at, 1, at, size)
        put(hold.at[1], at, 3, HALF + at, size)
    load_own.wait()
    for half in (0, HALF):
        for at, size in PIECES:
            put(logits, half + at, 0, half + at, size)

    def turn(j, carry):
        cols = pl.ds(pl.multiple_of(j * block, block), block)
        for i in range(whole_blocks):
            head_t[cols, pl.ds(i * 128, 128)] = head_v[pl.ds(i * 128, 128), cols].T
        head_t[cols, pl.ds(whole_blocks * 128, 128)] = tail[:, cols].T
        return carry

    lax.fori_loop(0, width // block, turn, 0)
    load_frozen.wait()
    for copy in load_rows[1:]:
        copy.wait()
    frozen_f[pl.ds(1184, ROWS - 1184)] = jnp.zeros((ROWS - 1184, frozen_f.shape[1]), F32)
    frozen_f[pl.ds(0, vocab_here)] = frozen_v[...].astype(F32)

    def add_into(dst, at, piece, parts):
        quarter = PIECES[piece][1] // 4
        for k, part in enumerate(parts):
            rows = pl.ds(at + k * quarter, quarter)
            dst[rows] = dst[rows] + part

    for piece, (at, size) in enumerate(PIECES):
        for slot in (0, 1):
            packed_copy(1, slot, piece).wait_recv()
            add_into(hold.at[slot], at, piece, read_packed(rcv1, slot, piece, ONE))
            send_packed(snd3, slot, piece, hold[slot, pl.ds(at, size)], TWO)
            packed_copy(2, slot, piece).start()

    heard(2)

    for slot in (0, 1):
        half = (HALF, 0)[slot]
        for piece, (at, size) in enumerate(PIECES):
            packed_copy(0, slot, piece).wait_recv()
            add_into(logits, half + at, piece, read_packed(rcv2, slot, piece, ONE))
    for piece, (at, size) in enumerate(PIECES):
        for slot in (0, 1):
            half = (0, HALF)[slot]
            packed_copy(2, slot, piece).wait_recv()
            add_into(logits, half + at, piece, read_packed(rcv3, slot, piece, TWO))

    edge = vocab_here // 8 * 8
    rows = edge + lax.broadcasted_iota(jnp.int32, (ROWS - edge, logits.shape[1]), 0)
    logits[pl.ds(edge, ROWS - edge)] = jnp.where(
        rows < vocab_here, logits[pl.ds(edge, ROWS - edge)], -1e30
    )

    step = ROWS // 4
    tops = [jnp.max(logits[pl.ds(k * step, step)], axis=0, keepdims=True) for k in range(4)]
    top = functools.reduce(jnp.maximum, tops)
    total = jnp.zeros_like(top)
    cross = jnp.zeros_like(top)
    for k in range(4):
        piece = pl.ds(k * step, step)
        shifted = jnp.exp(logits[piece] - top)
        total += jnp.sum(shifted, axis=0, keepdims=True)
        cross += jnp.sum(shifted * (logits[piece] - frozen_f[piece]), axis=0, keepdims=True)

    def exchange(top, total, cross, out, into, send, recv, to, count, meanwhile):
        out[0:1] = top
        out[1:2] = total
        out[2:3] = cross
        out[3:4] = cross

        def go(k, carry):
            remote(out, into.at[k], send.at[k], recv.at[k], to(k)).start()
            return carry

        def arrive(k, carry):
            remote(out, into.at[k], send.at[k], recv.at[k], to(k)).wait()
            return carry

        lax.fori_loop(1, count, go, 0)
        meanwhile()
        lax.fori_loop(1, count, arrive, 0)
        best = top
        for k in range(1, count):
            best = jnp.maximum(best, into[k, 0:1])
        scale = jnp.exp(top - best)
        all_total, all_cross = total * scale, cross * scale
        for k in range(1, count):
            scale = jnp.exp(into[k, 0:1] - best)
            all_total += into[k, 1:2] * scale
            all_cross += into[k, 2:3] * scale
        return best, all_total, all_cross

    top_here = top
    centre = cross / total

    def early_copy(slot, kind):
        device = ((right, left)[slot], v)
        half = (slot, 1 - slot, slot)[kind]
        source = ((0, 0, 3), (0, 0, 1))[slot][kind]
        into = ((3, 3, 2), (1, 1, 2))[slot][kind]
        sem = slot * 3 + kind
        return remote(
            eu.at[source, half], eu.at[into, half], e_send.at[sem], e_recv.at[sem], device
        )

    def send_early():
        for half in (0, 1):
            for k in (0, 1):
                at = k * (EARLY // 2)
                piece = pl.ds(half * HALF + at, EARLY // 2)
                value = logits[piece]
                shifted = jnp.exp(value - top_here)
                eu[0, half, pl.ds(at, EARLY // 2)] = shifted.astype(BF16)
                eu[0, half, pl.ds(EARLY + at, EARLY // 2)] = (
                    shifted * (value - frozen_f[piece] - centre)
                ).astype(BF16)
            early_copy(half, 0).start()
        early_copy(1, 1).start()
        early_copy(0, 1).start()

    def pass_early():
        for slot in (0, 1):
            early_copy(slot, 0).wait_recv()
            early_copy(slot, 2).start()

    top, total, cross = exchange(
        top, total, cross, st1, st1_in, s1_send, s1_recv, in_group, GROUP, send_early
    )
    top, total, cross = exchange(
        top, total, cross, st2, st2_in, s2_send, s2_recv, along_z, NZ, pass_early
    )
    mean = cross / total
    out_div[...] = mean - top - jnp.log(total) + norms[...]

    for copy in counts:
        copy.wait()
    all_counts = cnt[...] + cnt_in[0] + cnt_in[1] + cnt_in[2]
    weight = cnt[...] / jnp.sum(all_counts, axis=1, keepdims=True)
    adv, ratio = advantages[...], ratios[...]
    open_ = jnp.where(adv >= 0.0, (ratio <= 1.0 + clip_eps).astype(F32), (ratio >= 1.0 - clip_eps).astype(F32))
    policy = jnp.where(open_ > 0.5, -adv * ratio, jnp.zeros_like(ratio))
    target = targets[...] - v * vocab_here
    target = jnp.where(target < vocab_here, target, -1)
    inverse = 1.0 / total
    hits = weight * policy
    terms[0:1] = weight * jnp.exp(top_here - top) * inverse
    terms[1:2] = penalty * (mean - centre) + policy
    terms[2:3] = hits
    terms[3:4] = target.astype(F32)
    tell_terms = [
        remote(terms, terms_in.at[k - 1], t_send.at[k - 1], t_recv.at[k - 1], (lax.rem(me + k, 4), v))
        for k in (1, 2, 3)
    ]
    for copy in tell_terms:
        copy.start()

    def gradient_copy(slot, kind):
        device = ((right, left)[slot], v)
        half = (slot, 1 - slot, slot)[kind]
        rows = pl.ds(half * HALF + EARLY, LATE[half])
        source = ((0, 0, 3), (0, 0, 1))[slot][kind]
        into = ((3, 3, 2), (1, 1, 2))[slot][kind]
        sem = slot * 3 + kind
        return remote(g.at[source, rows], g.at[into, rows], g_send.at[sem], g_recv.at[sem], device)

    def own_gradient(at, size):
        piece = pl.ds(at, size)
        value = logits[piece]
        chance = jnp.exp(value - top) * inverse
        rows = at + lax.broadcasted_iota(jnp.int32, value.shape, 0)
        grad = weight * (penalty * chance * (value - frozen_f[piece] - mean) - policy * chance)
        grad = jnp.where(rows == target, grad + hits, grad)
        g[0, piece] = grad.astype(BF16)

    own_gradient(EARLY, HALF - EARLY)
    gradient_copy(0, 0).start()
    own_gradient(HALF + EARLY, HALF - EARLY)
    gradient_copy(1, 0).start()
    gradient_copy(1, 1).start()
    gradient_copy(0, 1).start()
    own_gradient(0, EARLY)
    own_gradient(HALF, EARLY)

    def early_gradient(r):
        alpha, kappa, hit, there = (terms_in[3 - r, k : k + 1] for k in range(4))
        there = there.astype(jnp.int32)
        for half in (0, 1):
            for k in (0, 1):
                at = k * (EARLY // 2)
                shifted = eu[r, half, pl.ds(at, EARLY // 2)].astype(F32)
                moved = eu[r, half, pl.ds(EARLY + at, EARLY // 2)].astype(F32)
                grad = alpha * (penalty * moved - kappa * shifted)
                at = half * HALF + at
                rows = at + lax.broadcasted_iota(jnp.int32, grad.shape, 0)
                grad = jnp.where(rows == there, grad + hit, grad)
                g[r, pl.ds(at, EARLY // 2)] = grad.astype(BF16)

    chunk = width // 4
    active = lax.rem(z, 2) == core
    sender = lax.rem(z, 2) != core

    def partial(sources):
        right_side = [g[r] for r in sources]
        right_side = right_side[0] if len(sources) == 1 else jnp.concatenate(right_side, axis=1)
        deep = NZ // 8
        for i in range(4):
            value = jnp.dot(head_t[pl.ds(i * chunk, chunk)], right_side, preferred_element_type=F32)
            for j, r in enumerate(sources):
                prod[r, pl.ds(i * deep, deep)] = value[:, j * 128 : (j + 1) * 128].reshape(
                    deep, 2, NX, 16, 128
                )
        for r in sources:
            pair(r).start()

    def pair(r):
        return remote(prod.at[r, :, 1 - core], prod_in.at[r], a_send.at[r], a_recv.at[r], sibling)

    def x_copy(r, k):
        sem = r * NX + k
        return remote(xs.at[r, k], xs_in.at[r, k], x_send.at[sem], x_recv.at[sem], along_x(k))

    def z_copy(r, k):
        m = lax.rem(z // 2 + k, NZ // 2)
        there = 2 * m + core
        slot = lax.rem(z - there + NZ, NZ)
        return remote(
            zs.at[r, m], zs_in.at[r, slot], z_send.at[r * NZ + k], z_recv.at[r * NZ + slot],
            (me, there * GROUP + xc),
        )

    def to_x(r):
        pair(r).wait_recv()
        for k in (*range(1, NX), 0):
            there = lax.rem(x + k, NX)
            value = prod[r, :, core, there] + prod_in[r, :, there]
            if k == 0:
                mid[r] = value
            else:
                xs[r, k] = value.reshape(NZ * 8, 128).astype(BF16)
                x_copy(r, k).start()

    def to_z(r):
        value = mid[r]
        for k in range(1, NX):
            x_copy(r, k).wait_recv()
            value = value + xs_in[r, k].astype(F32).reshape(NZ // 2, 16, 128)
        mid[r] = value
        zs[r] = value.astype(BF16)

        def go(k, carry):
            z_copy(r, k).start()
            return carry

        lax.fori_loop(1, NZ // 2, go, 0)

        @pl.when(sender)
        def _():
            z_copy(r, 0).start()

    def finish(r):
        def arrive(k, carry):
            remote(
                zs.at[r, 0], zs_in.at[r, k], z_send.at[r * NZ], z_recv.at[r * NZ + k],
                (me, lax.rem(z + k, NZ) * GROUP + xc),
            ).wait_recv()
            return carry

        lax.fori_loop(1, NZ, arrive, 0)
        value = mid[r, z // 2]
        for k in range(1, NZ):
            value = value + zs_in[r, k].astype(F32)
        tokens = pl.ds(pl.multiple_of(lax.rem(me + r, 4) * 128, 128), 128)
        total_h[0, :, tokens] = value[:8]
        total_h[1, :, tokens] = value[8:]

    last = remote(
        total_h.at[1 - core], total_h.at[1 - core], f_sem.at[0], f_sem.at[1], sibling
    )

    head_rows = ((0, 304), (304, 304), (608, 304), (912, vocab_here - 912))

    def head_gradient(k):
        at, size = head_rows[k]
        rows = pl.ds(at, size)
        left_side = jnp.concatenate([g[r, rows] for r in range(4)], axis=1)
        tokens = hid[...].reshape(4 * hid.shape[1], width)
        out_head[rows] = jnp.dot(left_side, tokens, preferred_element_type=F32).astype(BF16)

    partial((0,))
    for copy in tell_terms:
        copy.wait_recv()
    gradient_copy(0, 0).wait_recv()
    gradient_copy(0, 2).start()
    gradient_copy(1, 0).wait_recv()
    gradient_copy(1, 2).start()
    to_x(0)
    for slot in (0, 1):
        early_copy(slot, 1).wait_recv()
    early_gradient(1)
    early_gradient(3)
    gradient_copy(0, 1).wait_recv()
    gradient_copy(1, 1).wait_recv()
    partial((1, 3))
    to_z(0)
    for slot in (0, 1):
        early_copy(slot, 2).wait_recv()
    early_gradient(2)
    to_x(1)
    to_x(3)
    gradient_copy(0, 2).wait_recv()
    gradient_copy(1, 2).wait_recv()
    partial((2,))
    head_gradient(0)
    to_x(2)
    to_z(1)
    to_z(3)
    head_gradient(1)
    head_gradient(2)
    to_z(2)
    head_gradient(3)

    @pl.when(active)
    def _():
        for r in (0, 1, 3, 2):
            finish(r)
        last.start()
        last.wait_send()

    @pl.when(sender)
    def _():
        last.wait_recv()

    out_hidden[...] = total_h[core].astype(BF16)

    for copy in (h_right, h_left, h_far, h_on, share[1], share[2], share[3]):
        copy.wait_send()
    for stage in range(3):
        for slot in (0, 1):
            for piece in (0, 1):
                packed_copy(stage, slot, piece).wait_send()
    for slot in (0, 1):
        for kind in range(3):
            gradient_copy(slot, kind).wait_send()
            early_copy(slot, kind).wait_send()
    for copy in tell_terms:
        copy.wait_send()
    for r in range(4):
        pair(r).wait_send()
        for k in range(1, NX):
            x_copy(r, k).wait_send()

        def left_z(k, carry):
            z_copy(r, k).wait_send()
            return carry

        lax.fori_loop(1, NZ // 2, left_z, 0)

        @pl.when(sender)
        def _():
            z_copy(r, 0).wait_send()


def local(devices, hidden, head, frozen, norms, advantages, ratios, targets, counted):
    tokens, depth = hidden.shape
    width = depth // 4
    vocab_here = head.shape[1]
    NZ = devices // (2 * NX)
    GROUP = 2 * NX
    packed = pltpu.VMEM((2, HALF // 4 * 3, tokens), jnp.int32)
    dma = pltpu.SemaphoreType.DMA
    row = [a.reshape(1, tokens) for a in (norms, advantages, ratios, targets, counted)]
    vmem = pl.BlockSpec(memory_space=pltpu.VMEM)
    out = pl.pallas_call(
        functools.partial(kernel, devices),
        out_shape=(
            jax.ShapeDtypeStruct((width // devices, 4 * tokens), BF16),
            jax.ShapeDtypeStruct((vocab_here, width), BF16),
            jax.ShapeDtypeStruct((1, tokens), F32),
        ),
        in_specs=[pl.BlockSpec(memory_space=pltpu.HBM)] * 8,
        out_specs=(vmem, vmem, vmem),
        scratch_shapes=[
            pltpu.VMEM((1, tokens), F32),
            pltpu.VMEM((1, tokens), F32),
            pltpu.VMEM((1, tokens), F32),
            pltpu.VMEM((1, tokens), jnp.int32),
            pltpu.VMEM((1, tokens), jnp.int32),
            pltpu.VMEM((vocab_here, width), BF16),
            pltpu.VMEM((width, DEEP), BF16),
            pltpu.VMEM((128, width), BF16),
            pltpu.VMEM((vocab_here, tokens), BF16),
            pltpu.VMEM((ROWS, tokens), F32),
            pltpu.VMEM((4, tokens, width), BF16),
            pltpu.VMEM((tokens // 2, width), BF16),
            pltpu.VMEM((ROWS, tokens), F32),
            pltpu.VMEM((2, HALF, tokens), F32),
            packed, packed, packed, packed, packed, packed,
            pltpu.VMEM((1, tokens), F32),
            pltpu.VMEM((3, 1, tokens), F32),
            pltpu.VMEM((4, tokens), F32),
            pltpu.VMEM((GROUP, 4, tokens), F32),
            pltpu.VMEM((4, tokens), F32),
            pltpu.VMEM((NZ, 4, tokens), F32),
            pltpu.VMEM((4, 2, 2 * EARLY, tokens), BF16),
            pltpu.VMEM((4, tokens), F32),
            pltpu.VMEM((3, 4, tokens), F32),
            pltpu.VMEM((4, DEEP, tokens), BF16),
            pltpu.VMEM((4, NZ // 2, 2, NX, 16, tokens), F32),
            pltpu.VMEM((4, NZ // 2, NX, 16, tokens), F32),
            pltpu.VMEM((4, NZ // 2, 16, tokens), F32),
            pltpu.VMEM((4, NX, NZ * 8, tokens), BF16),
            pltpu.VMEM((4, NX, NZ * 8, tokens), BF16),
            pltpu.VMEM((4, NZ // 2, 16, tokens), BF16),
            pltpu.VMEM((4, NZ, 16, tokens), BF16),
            pltpu.VMEM((2, 8, 4 * tokens), F32),
            dma((8,)),
            dma((4,)), dma((4,)),
            dma((4,)), dma((4,)),
            dma((12,)), dma((12,)),
            dma((3,)), dma((3,)),
            dma((GROUP,)), dma((GROUP,)),
            dma((NZ,)), dma((NZ,)),
            dma((6,)), dma((6,)),
            dma((3,)), dma((3,)),
            dma((6,)), dma((6,)),
            dma((4,)), dma((4,)),
            dma((4 * NX,)), dma((4 * NX,)),
            dma((4 * NZ,)), dma((4 * NZ,)),
            dma((2,)),
            pltpu.SemaphoreType.REGULAR((3,)),
        ],
        compiler_params=pltpu.CompilerParams(
            collective_id=0, has_side_effects=True, vmem_limit_bytes=48 * 1024 * 1024
        ),
    )(*(pltpu.with_memory_space_constraint(a, pltpu.HBM) for a in (hidden, head.T, frozen.T, *row)))
    return out[0].T, out[1].T, out[2].reshape(tokens)


def solution(mesh):
    return jax.shard_map(
        functools.partial(local, mesh.shape["vocab"]),
        mesh=mesh,
        in_specs=(
            P("dp", None),
            P("dp", "vocab"),
            P("dp", "vocab"),
            P("dp"),
            P("dp"),
            P("dp"),
            P("dp"),
            P("dp"),
        ),
        out_specs=(P(None, ("dp", "vocab")), P("dp", "vocab"), P("dp")),
        check_vma=False,
    )
```

```python
import functools

import jax
import jax.numpy as jnp
from jax import lax
from jax.experimental import pallas as pl
from jax.experimental.pallas import tpu as pltpu
from jax.sharding import PartitionSpec as P

clip_eps = 0.2
penalty = 0.1

NX = 4
HALF = 608
PIECES = ((0, 320), (320, 288))
EARLY = 320
LATE = (288, 272)
ROWS = 2 * HALF
DEEP = 1280
ONE = 512.0
TWO = 256.0
MESH = pl.DeviceIdType.MESH
F32 = jnp.float32
BF16 = jnp.bfloat16


def pack(values, scale):
    top = 8388607.0
    whole = jnp.clip(jnp.floor(values * scale + 0.5), -top, top).astype(jnp.int32)
    quarter = values.shape[0] // 4
    a, b, c, d = (whole[k * quarter : (k + 1) * quarter] for k in range(4))
    low = 0xFFFFFF
    return (
        (a & low) | (d << 24),
        (b & low) | ((d >> 8) << 24),
        (c & low) | ((d >> 16) << 24),
    )


def unpack(u, v, w, scale):
    parts = [(word << 8) >> 8 for word in (u, v, w)]
    parts.append(((u >> 24) & 0xFF) | (((v >> 24) & 0xFF) << 8) | ((w >> 24) << 16))
    back = 1.0 / scale
    return [part.astype(F32) * back for part in parts]


def kernel(
    devices,
    hidden, head, frozen, norms_h, advantages_h, ratios_h, targets_h, counted_h,
    out_hidden, out_head, out_div,
    norms, advantages, ratios, targets, counted, head_v, head_t, tail, frozen_v, frozen_f, hid, via, logits, hold,
    snd2, snd1, snd3, rcv2, rcv1, rcv3,
    cnt, cnt_in, st1, st1_in, st2, st2_in,
    eu, terms, terms_in, g, prod, prod_in, mid, xs, xs_in, zs, zs_in, total_h,
    load_sem, h_send, h_recv, sh_send, sh_recv, r_send, r_recv,
    c_send, c_recv, s1_send, s1_recv, s2_send, s2_recv,
    e_send, e_recv, t_send, t_recv, g_send, g_recv, a_send, a_recv, x_send, x_recv, z_send, z_recv, f_sem, hello,
):
    NZ = devices // (2 * NX)
    GROUP = 2 * NX
    width = hid.shape[2]
    vocab_here = head.shape[0]
    me = lax.axis_index("dp")
    v = lax.axis_index("vocab")
    core = lax.rem(v, 2)
    x = lax.rem(v // 2, NX)
    z = v // GROUP
    xc = lax.rem(v, GROUP)
    right, far, left = (lax.rem(me + k, 4) for k in (1, 2, 3))
    sibling = (me, v + 1 - 2 * core)

    def in_group(k):
        return (me, z * GROUP + lax.rem(xc + k, GROUP))

    def along_x(k):
        return (me, z * GROUP + lax.rem(x + k, NX) * 2 + core)

    def along_z(k):
        return (me, lax.rem(z + k, NZ) * GROUP + xc)

    def remote(src, dst, send, recv, device):
        return pltpu.make_async_remote_copy(
            src_ref=src, dst_ref=dst, send_sem=send, recv_sem=recv,
            device_id=device, device_id_type=MESH,
        )

    def lanes(block):
        return pl.ds(pl.multiple_of(block * width, width), width)

    half_tok = hid.shape[1] // 2
    mine = pl.ds(pl.multiple_of(core * half_tok, half_tok), half_tok)

    load_head = pltpu.make_async_copy(head, head_v, load_sem.at[0])
    load_own = pltpu.make_async_copy(hidden.at[:, lanes(me)], hid.at[0], load_sem.at[1])
    load_frozen = pltpu.make_async_copy(frozen, frozen_v, load_sem.at[2])
    load_rows = [
        pltpu.make_async_copy(src, dst, load_sem.at[3 + k])
        for k, (src, dst) in enumerate((
            (counted_h, counted), (norms_h, norms), (advantages_h, advantages),
            (ratios_h, ratios), (targets_h, targets),
        ))
    ]
    load_rows[0].start()
    load_head.start()
    load_own.start()
    load_frozen.start()
    for copy in load_rows[1:]:
        copy.start()
    barrier = pltpu.get_barrier_semaphore()

    near_y = [(lax.rem(me + k, 4), v) for k in (1, 3)]
    near_x = [along_x(k) for k in (1, NX - 1)] if NX > 1 else []

    def near_z(k):
        return [along_z(k), along_z(NZ - k)]

    nearest = [sibling, *near_y, *near_x, *near_z(1)]
    for device in nearest:
        pl.semaphore_signal(barrier, inc=1, device_id=device, device_id_type=MESH)
    rounds = (near_y + near_x + near_z(1), near_x + near_z(2), near_z(4))

    def tell(n):
        for device in rounds[n]:
            pl.semaphore_signal(hello.at[n], inc=1, device_id=device, device_id_type=MESH)

    def heard(n):
        pl.semaphore_wait(hello.at[n], len(rounds[n]))

    load_rows[0].wait()
    cnt[...] = counted[...].astype(F32)
    pl.semaphore_wait(barrier, len(nearest))

    onward = (lax.rem(me + 1 + 2 * core, 4), v)
    h_right = remote(hidden.at[mine, lanes(right)], hid.at[3, mine], h_send.at[0], h_recv.at[0], (right, v))
    h_left = remote(hidden.at[mine, lanes(left)], hid.at[1, mine], h_send.at[1], h_recv.at[1], (left, v))
    h_far = remote(hidden.at[mine, lanes(far)], via, h_send.at[2], h_recv.at[2], onward)
    h_on = remote(via, hid.at[2, mine], h_send.at[3], h_recv.at[3], onward)
    h_right.start()
    h_left.start()
    h_far.start()
    counts = [
        remote(cnt, cnt_in.at[k - 1], c_send.at[k - 1], c_recv.at[k - 1], (lax.rem(me + k, 4), v))
        for k in (1, 2, 3)
    ]
    tell(0)
    share = {
        r: remote(hid.at[r, mine], hid.at[r, mine], sh_send.at[r], sh_recv.at[r], sibling)
        for r in (1, 2, 3)
    }

    for r in range(4):
        g[r, pl.ds(1184, DEEP - 1184)] = jnp.zeros((DEEP - 1184, g.shape[2]), BF16)
    tail[...] = jnp.zeros_like(tail)
    load_head.wait()

    def product(r, start, size):
        valid = min(size, vocab_here - start)
        rows = head_v[pl.ds(start, valid)]
        return valid, lax.dot_general(
            rows, hid[r], (((1,), (1,)), ((), ())), preferred_element_type=F32
        )

    def put(dst, at, r, start, size):
        valid, value = product(r, start, size)
        if valid < size:
            floor = valid // 8 * 8
            dst[pl.ds(at + floor, size - floor)] = jnp.zeros((size - floor, value.shape[1]), F32)
        dst[pl.ds(at, valid)] = value

    def send_packed(buffer, slot, piece, values, scale):
        at, size = PIECES[piece]
        quarter, at = size // 4, at // 4 * 3
        for k, words in enumerate(pack(values, scale)):
            buffer[slot, pl.ds(at + k * quarter, quarter)] = words

    def read_packed(buffer, slot, piece, scale):
        at, size = PIECES[piece]
        quarter, at = size // 4, at // 4 * 3
        return unpack(*(buffer[slot, pl.ds(at + k * quarter, quarter)] for k in range(3)), scale)

    def packed_copy(step, slot, piece):
        snd, rcv = ((snd2, rcv2), (snd1, rcv1), (snd3, rcv3))[step]
        at, size = PIECES[piece]
        rows = pl.ds(at // 4 * 3, size // 4 * 3)
        sem = (step * 2 + slot) * 2 + piece
        return remote(
            snd.at[slot, rows], rcv.at[slot, rows], r_send.at[sem], r_recv.at[sem],
            ((right, left)[slot], v),
        )

    h_left.wait_recv()
    share[1].start()
    h_right.wait_recv()
    share[3].start()
    h_far.wait_recv()
    h_on.start()

    heard(0)
    tell(1)
    for copy in counts:
        copy.start()

    block = min(128, width)
    whole_blocks = vocab_here // 128
    tail[pl.ds(0, vocab_here - whole_blocks * 128)] = head_v[pl.ds(whole_blocks * 128, vocab_here - whole_blocks * 128)]

    share[1].wait_recv()
    for piece, (at, size) in enumerate(PIECES):
        put(hold.at[0], at, 1, HALF + at, size)
        send_packed(snd2, 0, piece, hold[0, pl.ds(at, size)], ONE)
        packed_copy(0, 0, piece).start()
    share[3].wait_recv()
    for piece, (at, size) in enumerate(PIECES):
        put(hold.at[1], at, 3, at, size)
        send_packed(snd2, 1, piece, hold[1, pl.ds(at, size)], ONE)
        packed_copy(0, 1, piece).start()

    heard(1)
    tell(2)

    h_on.wait_recv()
    share[2].start()
    share[2].wait_recv()
    for piece, (at, size) in enumerate(PIECES):
        put(hold.at[0], at, 2, at, size)
        send_packed(snd1, 0, piece, hold[0, pl.ds(at, size)], ONE)
        packed_copy(1, 0, piece).start()
        put(hold.at[1], at, 2, HALF + at, size)
        send_packed(snd1, 1, piece, hold[1, pl.ds(at, size)], ONE)
        packed_copy(1, 1, piece).start()

    for at, size in PIECES:
        put(hold.at[0], at, 1, at, size)
        put(hold.at[1], at, 3, HALF + at, size)
    load_own.wait()
    for half in (0, HALF):
        for at, size in PIECES:
            put(logits, half + at, 0, half + at, size)

    def turn(j, carry):
        cols = pl.ds(pl.multiple_of(j * block, block), block)
        for i in range(whole_blocks):
            head_t[cols, pl.ds(i * 128, 128)] = head_v[pl.ds(i * 128, 128), cols].T
        head_t[cols, pl.ds(whole_blocks * 128, 128)] = tail[:, cols].T
        return carry

    lax.fori_loop(0, width // block, turn, 0)
    load_frozen.wait()
    for copy in load_rows[1:]:
        copy.wait()
    frozen_f[pl.ds(1184, ROWS - 1184)] = jnp.zeros((ROWS - 1184, frozen_f.shape[1]), F32)
    frozen_f[pl.ds(0, vocab_here)] = frozen_v[...].astype(F32)

    def add_into(dst, at, piece, parts):
        quarter = PIECES[piece][1] // 4
        for k, part in enumerate(parts):
            rows = pl.ds(at + k * quarter, quarter)
            dst[rows] = dst[rows] + part

    for piece, (at, size) in enumerate(PIECES):
        for slot in (0, 1):
            packed_copy(1, slot, piece).wait_recv()
            add_into(hold.at[slot], at, piece, read_packed(rcv1, slot, piece, ONE))
            send_packed(snd3, slot, piece, hold[slot, pl.ds(at, size)], TWO)
            packed_copy(2, slot, piece).start()

    heard(2)

    for slot in (0, 1):
        half = (HALF, 0)[slot]
        for piece, (at, size) in enumerate(PIECES):
            packed_copy(0, slot, piece).wait_recv()
            add_into(logits, half + at, piece, read_packed(rcv2, slot, piece, ONE))
    for piece, (at, size) in enumerate(PIECES):
        for slot in (0, 1):
            half = (0, HALF)[slot]
            packed_copy(2, slot, piece).wait_recv()
            add_into(logits, half + at, piece, read_packed(rcv3, slot, piece, TWO))

    edge = vocab_here // 8 * 8
    rows = edge + lax.broadcasted_iota(jnp.int32, (ROWS - edge, logits.shape[1]), 0)
    logits[pl.ds(edge, ROWS - edge)] = jnp.where(
        rows < vocab_here, logits[pl.ds(edge, ROWS - edge)], -1e30
    )

    step = ROWS // 4
    tops = [jnp.max(logits[pl.ds(k * step, step)], axis=0, keepdims=True) for k in range(4)]
    top = functools.reduce(jnp.maximum, tops)
    total = jnp.zeros_like(top)
    cross = jnp.zeros_like(top)
    for k in range(4):
        piece = pl.ds(k * step, step)
        shifted = jnp.exp(logits[piece] - top)
        total += jnp.sum(shifted, axis=0, keepdims=True)
        cross += jnp.sum(shifted * (logits[piece] - frozen_f[piece]), axis=0, keepdims=True)

    def far_first(i, count):
        return count // 2 + (1 - 2 * lax.rem(i, 2)) * ((i + 1) // 2)

    def exchange(top, total, cross, out, into, send, recv, to, count, meanwhile):
        out[0:1] = top
        out[1:2] = total
        out[2:3] = cross
        out[3:4] = cross

        def go(i, carry):
            k = far_first(i, count)
            remote(out, into.at[k], send.at[k], recv.at[k], to(k)).start()
            return carry

        def arrive(k, carry):
            remote(out, into.at[k], send.at[k], recv.at[k], to(k)).wait()
            return carry

        lax.fori_loop(0, count - 1, go, 0)
        meanwhile()
        lax.fori_loop(1, count, arrive, 0)
        best = top
        for k in range(1, count):
            best = jnp.maximum(best, into[k, 0:1])
        scale = jnp.exp(top - best)
        all_total, all_cross = total * scale, cross * scale
        for k in range(1, count):
            scale = jnp.exp(into[k, 0:1] - best)
            all_total += into[k, 1:2] * scale
            all_cross += into[k, 2:3] * scale
        return best, all_total, all_cross

    top_here = top
    centre = cross / total

    def early_copy(slot, kind):
        device = ((right, left)[slot], v)
        half = (slot, 1 - slot, slot)[kind]
        source = ((0, 0, 3), (0, 0, 1))[slot][kind]
        into = ((3, 3, 2), (1, 1, 2))[slot][kind]
        sem = slot * 3 + kind
        return remote(
            eu.at[source, half], eu.at[into, half], e_send.at[sem], e_recv.at[sem], device
        )

    def send_early():
        for half in (0, 1):
            for k in (0, 1):
                at = k * (EARLY // 2)
                piece = pl.ds(half * HALF + at, EARLY // 2)
                value = logits[piece]
                shifted = jnp.exp(value - top_here)
                eu[0, half, pl.ds(at, EARLY // 2)] = shifted.astype(BF16)
                eu[0, half, pl.ds(EARLY + at, EARLY // 2)] = (
                    shifted * (value - frozen_f[piece] - centre)
                ).astype(BF16)
            early_copy(half, 0).start()
        early_copy(1, 1).start()
        early_copy(0, 1).start()

    def pass_early():
        for slot in (0, 1):
            early_copy(slot, 0).wait_recv()
            early_copy(slot, 2).start()

    top, total, cross = exchange(
        top, total, cross, st1, st1_in, s1_send, s1_recv, in_group, GROUP, send_early
    )
    top, total, cross = exchange(
        top, total, cross, st2, st2_in, s2_send, s2_recv, along_z, NZ, pass_early
    )
    mean = cross / total
    out_div[...] = mean - top - jnp.log(total) + norms[...]

    for copy in counts:
        copy.wait()
    all_counts = cnt[...] + cnt_in[0] + cnt_in[1] + cnt_in[2]
    weight = cnt[...] / jnp.sum(all_counts, axis=1, keepdims=True)
    adv, ratio = advantages[...], ratios[...]
    open_ = jnp.where(adv >= 0.0, (ratio <= 1.0 + clip_eps).astype(F32), (ratio >= 1.0 - clip_eps).astype(F32))
    policy = jnp.where(open_ > 0.5, -adv * ratio, jnp.zeros_like(ratio))
    target = targets[...] - v * vocab_here
    target = jnp.where(target < vocab_here, target, -1)
    inverse = 1.0 / total
    hits = weight * policy
    terms[0:1] = weight * jnp.exp(top_here - top) * inverse
    terms[1:2] = penalty * (mean - centre) + policy
    terms[2:3] = hits
    terms[3:4] = target.astype(F32)
    tell_terms = [
        remote(terms, terms_in.at[k - 1], t_send.at[k - 1], t_recv.at[k - 1], (lax.rem(me + k, 4), v))
        for k in (1, 2, 3)
    ]
    for copy in tell_terms:
        copy.start()

    def gradient_copy(slot, kind):
        device = ((right, left)[slot], v)
        half = (slot, 1 - slot, slot)[kind]
        rows = pl.ds(half * HALF + EARLY, LATE[half])
        source = ((0, 0, 3), (0, 0, 1))[slot][kind]
        into = ((3, 3, 2), (1, 1, 2))[slot][kind]
        sem = slot * 3 + kind
        return remote(g.at[source, rows], g.at[into, rows], g_send.at[sem], g_recv.at[sem], device)

    def own_gradient(at, size):
        piece = pl.ds(at, size)
        value = logits[piece]
        chance = jnp.exp(value - top) * inverse
        rows = at + lax.broadcasted_iota(jnp.int32, value.shape, 0)
        grad = weight * (penalty * chance * (value - frozen_f[piece] - mean) - policy * chance)
        grad = jnp.where(rows == target, grad + hits, grad)
        g[0, piece] = grad.astype(BF16)

    own_gradient(EARLY, HALF - EARLY)
    gradient_copy(0, 0).start()
    own_gradient(HALF + EARLY, HALF - EARLY)
    gradient_copy(1, 0).start()
    gradient_copy(1, 1).start()
    gradient_copy(0, 1).start()
    own_gradient(0, EARLY)
    own_gradient(HALF, EARLY)

    def early_gradient(r):
        alpha, kappa, hit, there = (terms_in[3 - r, k : k + 1] for k in range(4))
        there = there.astype(jnp.int32)
        for half in (0, 1):
            for k in (0, 1):
                at = k * (EARLY // 2)
                shifted = eu[r, half, pl.ds(at, EARLY // 2)].astype(F32)
                moved = eu[r, half, pl.ds(EARLY + at, EARLY // 2)].astype(F32)
                grad = alpha * (penalty * moved - kappa * shifted)
                at = half * HALF + at
                rows = at + lax.broadcasted_iota(jnp.int32, grad.shape, 0)
                grad = jnp.where(rows == there, grad + hit, grad)
                g[r, pl.ds(at, EARLY // 2)] = grad.astype(BF16)

    chunk = width // 4
    active = lax.rem(z, 2) == core
    sender = lax.rem(z, 2) != core

    def partial(sources):
        right_side = [g[r] for r in sources]
        right_side = right_side[0] if len(sources) == 1 else jnp.concatenate(right_side, axis=1)
        deep = NZ // 8
        for i in range(4):
            value = jnp.dot(head_t[pl.ds(i * chunk, chunk)], right_side, preferred_element_type=F32)
            for j, r in enumerate(sources):
                prod[r, pl.ds(i * deep, deep)] = value[:, j * 128 : (j + 1) * 128].reshape(
                    deep, 2, NX, 16, 128
                )
        for r in sources:
            pair(r).start()

    def pair(r):
        return remote(prod.at[r, :, 1 - core], prod_in.at[r], a_send.at[r], a_recv.at[r], sibling)

    def x_copy(r, k):
        sem = r * NX + k
        return remote(xs.at[r, k], xs_in.at[r, k], x_send.at[sem], x_recv.at[sem], along_x(k))

    def z_copy(r, k):
        m = lax.rem(z // 2 + k, NZ // 2)
        there = 2 * m + core
        slot = lax.rem(z - there + NZ, NZ)
        return remote(
            zs.at[r, m], zs_in.at[r, slot], z_send.at[r * NZ + k], z_recv.at[r * NZ + slot],
            (me, there * GROUP + xc),
        )

    def to_x(r):
        pair(r).wait_recv()
        for k in (*sorted(range(1, NX), key=lambda k: -min(k, NX - k)), 0):
            there = lax.rem(x + k, NX)
            value = prod[r, :, core, there] + prod_in[r, :, there]
            if k == 0:
                mid[r] = value
            else:
                xs[r, k] = value.reshape(NZ * 8, 128).astype(BF16)
                x_copy(r, k).start()

    def to_z(r):
        value = mid[r]
        for k in range(1, NX):
            x_copy(r, k).wait_recv()
            value = value + xs_in[r, k].astype(F32).reshape(NZ // 2, 16, 128)
        mid[r] = value
        zs[r] = value.astype(BF16)

        def go(i, carry):
            z_copy(r, far_first(i, NZ // 2)).start()
            return carry

        lax.fori_loop(0, NZ // 2 - 1, go, 0)

        @pl.when(sender)
        def _():
            z_copy(r, 0).start()

    def finish(r):
        def arrive(k, carry):
            remote(
                zs.at[r, 0], zs_in.at[r, k], z_send.at[r * NZ], z_recv.at[r * NZ + k],
                (me, lax.rem(z + k, NZ) * GROUP + xc),
            ).wait_recv()
            return carry

        lax.fori_loop(1, NZ, arrive, 0)
        value = mid[r, z // 2]
        for k in range(1, NZ):
            value = value + zs_in[r, k].astype(F32)
        tokens = pl.ds(pl.multiple_of(lax.rem(me + r, 4) * 128, 128), 128)
        total_h[0, :, tokens] = value[:8]
        total_h[1, :, tokens] = value[8:]

    last = remote(
        total_h.at[1 - core], total_h.at[1 - core], f_sem.at[0], f_sem.at[1], sibling
    )

    head_rows = ((0, 304), (304, 304), (608, 304), (912, vocab_here - 912))

    def head_gradient(k):
        at, size = head_rows[k]
        rows = pl.ds(at, size)
        left_side = jnp.concatenate([g[r, rows] for r in range(4)], axis=1)
        tokens = hid[...].reshape(4 * hid.shape[1], width)
        out_head[rows] = jnp.dot(left_side, tokens, preferred_element_type=F32).astype(BF16)

    partial((0,))
    for copy in tell_terms:
        copy.wait_recv()
    gradient_copy(0, 0).wait_recv()
    gradient_copy(0, 2).start()
    gradient_copy(1, 0).wait_recv()
    gradient_copy(1, 2).start()
    to_x(0)
    for slot in (0, 1):
        early_copy(slot, 1).wait_recv()
    early_gradient(1)
    early_gradient(3)
    gradient_copy(0, 1).wait_recv()
    gradient_copy(1, 1).wait_recv()
    partial((1, 3))
    to_z(0)
    for slot in (0, 1):
        early_copy(slot, 2).wait_recv()
    early_gradient(2)
    to_x(1)
    to_x(3)
    gradient_copy(0, 2).wait_recv()
    gradient_copy(1, 2).wait_recv()
    partial((2,))
    head_gradient(0)
    to_x(2)
    to_z(1)
    to_z(3)
    head_gradient(1)
    head_gradient(2)
    to_z(2)
    head_gradient(3)

    @pl.when(active)
    def _():
        for r in (0, 1, 3, 2):
            finish(r)
        last.start()
        last.wait_send()

    @pl.when(sender)
    def _():
        last.wait_recv()

    out_hidden[...] = total_h[core].astype(BF16)

    for copy in (h_right, h_left, h_far, h_on, share[1], share[2], share[3]):
        copy.wait_send()
    for stage in range(3):
        for slot in (0, 1):
            for piece in (0, 1):
                packed_copy(stage, slot, piece).wait_send()
    for slot in (0, 1):
        for kind in range(3):
            gradient_copy(slot, kind).wait_send()
            early_copy(slot, kind).wait_send()
    for copy in tell_terms:
        copy.wait_send()
    for r in range(4):
        pair(r).wait_send()
        for k in range(1, NX):
            x_copy(r, k).wait_send()

        def left_z(k, carry):
            z_copy(r, k).wait_send()
            return carry

        lax.fori_loop(1, NZ // 2, left_z, 0)

        @pl.when(sender)
        def _():
            z_copy(r, 0).wait_send()


def local(devices, hidden, head, frozen, norms, advantages, ratios, targets, counted):
    tokens, depth = hidden.shape
    width = depth // 4
    vocab_here = head.shape[1]
    NZ = devices // (2 * NX)
    GROUP = 2 * NX
    packed = pltpu.VMEM((2, HALF // 4 * 3, tokens), jnp.int32)
    dma = pltpu.SemaphoreType.DMA
    row = [a.reshape(1, tokens) for a in (norms, advantages, ratios, targets, counted)]
    vmem = pl.BlockSpec(memory_space=pltpu.VMEM)
    out = pl.pallas_call(
        functools.partial(kernel, devices),
        out_shape=(
            jax.ShapeDtypeStruct((width // devices, 4 * tokens), BF16),
            jax.ShapeDtypeStruct((vocab_here, width), BF16),
            jax.ShapeDtypeStruct((1, tokens), F32),
        ),
        in_specs=[pl.BlockSpec(memory_space=pltpu.HBM)] * 8,
        out_specs=(vmem, vmem, vmem),
        scratch_shapes=[
            pltpu.VMEM((1, tokens), F32),
            pltpu.VMEM((1, tokens), F32),
            pltpu.VMEM((1, tokens), F32),
            pltpu.VMEM((1, tokens), jnp.int32),
            pltpu.VMEM((1, tokens), jnp.int32),
            pltpu.VMEM((vocab_here, width), BF16),
            pltpu.VMEM((width, DEEP), BF16),
            pltpu.VMEM((128, width), BF16),
            pltpu.VMEM((vocab_here, tokens), BF16),
            pltpu.VMEM((ROWS, tokens), F32),
            pltpu.VMEM((4, tokens, width), BF16),
            pltpu.VMEM((tokens // 2, width), BF16),
            pltpu.VMEM((ROWS, tokens), F32),
            pltpu.VMEM((2, HALF, tokens), F32),
            packed, packed, packed, packed, packed, packed,
            pltpu.VMEM((1, tokens), F32),
            pltpu.VMEM((3, 1, tokens), F32),
            pltpu.VMEM((4, tokens), F32),
            pltpu.VMEM((GROUP, 4, tokens), F32),
            pltpu.VMEM((4, tokens), F32),
            pltpu.VMEM((NZ, 4, tokens), F32),
            pltpu.VMEM((4, 2, 2 * EARLY, tokens), BF16),
            pltpu.VMEM((4, tokens), F32),
            pltpu.VMEM((3, 4, tokens), F32),
            pltpu.VMEM((4, DEEP, tokens), BF16),
            pltpu.VMEM((4, NZ // 2, 2, NX, 16, tokens), F32),
            pltpu.VMEM((4, NZ // 2, NX, 16, tokens), F32),
            pltpu.VMEM((4, NZ // 2, 16, tokens), F32),
            pltpu.VMEM((4, NX, NZ * 8, tokens), BF16),
            pltpu.VMEM((4, NX, NZ * 8, tokens), BF16),
            pltpu.VMEM((4, NZ // 2, 16, tokens), BF16),
            pltpu.VMEM((4, NZ, 16, tokens), BF16),
            pltpu.VMEM((2, 8, 4 * tokens), F32),
            dma((8,)),
            dma((4,)), dma((4,)),
            dma((4,)), dma((4,)),
            dma((12,)), dma((12,)),
            dma((3,)), dma((3,)),
            dma((GROUP,)), dma((GROUP,)),
            dma((NZ,)), dma((NZ,)),
            dma((6,)), dma((6,)),
            dma((3,)), dma((3,)),
            dma((6,)), dma((6,)),
            dma((4,)), dma((4,)),
            dma((4 * NX,)), dma((4 * NX,)),
            dma((4 * NZ,)), dma((4 * NZ,)),
            dma((2,)),
            pltpu.SemaphoreType.REGULAR((3,)),
        ],
        compiler_params=pltpu.CompilerParams(
            collective_id=0, has_side_effects=True, vmem_limit_bytes=48 * 1024 * 1024
        ),
    )(*(pltpu.with_memory_space_constraint(a, pltpu.HBM) for a in (hidden, head.T, frozen.T, *row)))
    return out[0].T, out[1].T, out[2].reshape(tokens)


def solution(mesh):
    return jax.shard_map(
        functools.partial(local, mesh.shape["vocab"]),
        mesh=mesh,
        in_specs=(
            P("dp", None),
            P("dp", "vocab"),
            P("dp", "vocab"),
            P("dp"),
            P("dp"),
            P("dp"),
            P("dp"),
            P("dp"),
        ),
        out_specs=(P(None, ("dp", "vocab")), P("dp", "vocab"), P("dp")),
        check_vma=False,
    )
```

```python
import functools

import jax
import jax.numpy as jnp
from jax import lax
from jax.experimental import pallas as pl
from jax.experimental.pallas import tpu as pltpu
from jax.sharding import PartitionSpec as P

clip_eps = 0.2
penalty = 0.1

NX = 4
HALF = 608
PIECES = ((0, 352), (352, 256))
EARLY = 320
LATE = (288, 272)
ROWS = 2 * HALF
DEEP = 1280
ONE = 512.0
TWO = 256.0
MESH = pl.DeviceIdType.MESH
F32 = jnp.float32
BF16 = jnp.bfloat16


def pack(values, scale):
    top = 8388607.0
    whole = jnp.clip(jnp.floor(values * scale + 0.5), -top, top).astype(jnp.int32)
    quarter = values.shape[0] // 4
    a, b, c, d = (whole[k * quarter : (k + 1) * quarter] for k in range(4))
    low = 0xFFFFFF
    return (
        (a & low) | (d << 24),
        (b & low) | ((d >> 8) << 24),
        (c & low) | ((d >> 16) << 24),
    )


def unpack(u, v, w, scale):
    parts = [(word << 8) >> 8 for word in (u, v, w)]
    parts.append(((u >> 24) & 0xFF) | (((v >> 24) & 0xFF) << 8) | ((w >> 24) << 16))
    back = 1.0 / scale
    return [part.astype(F32) * back for part in parts]


def kernel(
    devices,
    hidden, head, frozen, norms_h, advantages_h, ratios_h, targets_h, counted_h,
    out_hidden, out_head, out_div,
    norms, advantages, ratios, targets, counted, head_v, head_t, tail, frozen_v, frozen_f, hid, via, logits, hold,
    snd2, snd1, snd3, rcv2, rcv1, rcv3,
    cnt, cnt_in, st1, st1_in, st2, st2_in,
    eu, terms, terms_in, g, prod, prod_in, mid, xs, xs_in, zs, zs_in, total_h,
    load_sem, h_send, h_recv, sh_send, sh_recv, r_send, r_recv,
    c_send, c_recv, s1_send, s1_recv, s2_send, s2_recv,
    e_send, e_recv, t_send, t_recv, g_send, g_recv, a_send, a_recv, x_send, x_recv, z_send, z_recv, f_sem, hello,
):
    NZ = devices // (2 * NX)
    GROUP = 2 * NX
    width = hid.shape[2]
    vocab_here = head.shape[0]
    me = lax.axis_index("dp")
    v = lax.axis_index("vocab")
    core = lax.rem(v, 2)
    x = lax.rem(v // 2, NX)
    z = v // GROUP
    xc = lax.rem(v, GROUP)
    right, far, left = (lax.rem(me + k, 4) for k in (1, 2, 3))
    sibling = (me, v + 1 - 2 * core)

    def in_group(k):
        return (me, z * GROUP + lax.rem(xc + k, GROUP))

    def along_x(k):
        return (me, z * GROUP + lax.rem(x + k, NX) * 2 + core)

    def along_z(k):
        return (me, lax.rem(z + k, NZ) * GROUP + xc)

    def remote(src, dst, send, recv, device):
        return pltpu.make_async_remote_copy(
            src_ref=src, dst_ref=dst, send_sem=send, recv_sem=recv,
            device_id=device, device_id_type=MESH,
        )

    def lanes(block):
        return pl.ds(pl.multiple_of(block * width, width), width)

    half_tok = hid.shape[1] // 2
    mine = pl.ds(pl.multiple_of(core * half_tok, half_tok), half_tok)

    load_head = pltpu.make_async_copy(head, head_v, load_sem.at[0])
    load_own = pltpu.make_async_copy(hidden.at[:, lanes(me)], hid.at[0], load_sem.at[1])
    load_frozen = pltpu.make_async_copy(frozen, frozen_v, load_sem.at[2])
    load_rows = [
        pltpu.make_async_copy(src, dst, load_sem.at[3 + k])
        for k, (src, dst) in enumerate((
            (counted_h, counted), (norms_h, norms), (advantages_h, advantages),
            (ratios_h, ratios), (targets_h, targets),
        ))
    ]
    load_rows[0].start()
    load_head.start()
    load_own.start()
    load_frozen.start()
    for copy in load_rows[1:]:
        copy.start()
    barrier = pltpu.get_barrier_semaphore()

    near_y = [(lax.rem(me + k, 4), v) for k in (1, 3)]
    near_x = [along_x(k) for k in (1, NX - 1)] if NX > 1 else []

    def near_z(k):
        return [along_z(k), along_z(NZ - k)]

    nearest = [sibling, *near_y, *near_x, *near_z(1)]
    for device in nearest:
        pl.semaphore_signal(barrier, inc=1, device_id=device, device_id_type=MESH)
    rounds = (near_y + near_x + near_z(1), near_x + near_z(2), near_z(4))

    def tell(n):
        for device in rounds[n]:
            pl.semaphore_signal(hello.at[n], inc=1, device_id=device, device_id_type=MESH)

    def heard(n):
        pl.semaphore_wait(hello.at[n], len(rounds[n]))

    load_rows[0].wait()
    cnt[...] = counted[...].astype(F32)
    pl.semaphore_wait(barrier, len(nearest))

    onward = (lax.rem(me + 1 + 2 * core, 4), v)
    h_right = remote(hidden.at[mine, lanes(right)], hid.at[3, mine], h_send.at[0], h_recv.at[0], (right, v))
    h_left = remote(hidden.at[mine, lanes(left)], hid.at[1, mine], h_send.at[1], h_recv.at[1], (left, v))
    h_far = remote(hidden.at[mine, lanes(far)], via, h_send.at[2], h_recv.at[2], onward)
    h_on = remote(via, hid.at[2, mine], h_send.at[3], h_recv.at[3], onward)
    h_right.start()
    h_left.start()
    h_far.start()
    counts = [
        remote(cnt, cnt_in.at[k - 1], c_send.at[k - 1], c_recv.at[k - 1], (lax.rem(me + k, 4), v))
        for k in (1, 2, 3)
    ]
    tell(0)
    share = {
        r: remote(hid.at[r, mine], hid.at[r, mine], sh_send.at[r], sh_recv.at[r], sibling)
        for r in (1, 2, 3)
    }

    for r in range(4):
        g[r, pl.ds(1184, DEEP - 1184)] = jnp.zeros((DEEP - 1184, g.shape[2]), BF16)
    tail[...] = jnp.zeros_like(tail)
    load_head.wait()

    def product(r, start, size):
        valid = min(size, vocab_here - start)
        rows = head_v[pl.ds(start, valid)]
        return valid, lax.dot_general(
            rows, hid[r], (((1,), (1,)), ((), ())), preferred_element_type=F32
        )

    def put(dst, at, r, start, size):
        valid, value = product(r, start, size)
        if valid < size:
            floor = valid // 8 * 8
            dst[pl.ds(at + floor, size - floor)] = jnp.zeros((size - floor, value.shape[1]), F32)
        dst[pl.ds(at, valid)] = value

    def send_packed(buffer, slot, piece, values, scale):
        at, size = PIECES[piece]
        quarter, at = size // 4, at // 4 * 3
        for k, words in enumerate(pack(values, scale)):
            buffer[slot, pl.ds(at + k * quarter, quarter)] = words

    def read_packed(buffer, slot, piece, scale):
        at, size = PIECES[piece]
        quarter, at = size // 4, at // 4 * 3
        return unpack(*(buffer[slot, pl.ds(at + k * quarter, quarter)] for k in range(3)), scale)

    def packed_copy(step, slot, piece):
        snd, rcv = ((snd2, rcv2), (snd1, rcv1), (snd3, rcv3))[step]
        at, size = PIECES[piece]
        rows = pl.ds(at // 4 * 3, size // 4 * 3)
        sem = (step * 2 + slot) * 2 + piece
        return remote(
            snd.at[slot, rows], rcv.at[slot, rows], r_send.at[sem], r_recv.at[sem],
            ((right, left)[slot], v),
        )

    h_left.wait_recv()
    share[1].start()
    h_right.wait_recv()
    share[3].start()
    h_far.wait_recv()
    h_on.start()

    heard(0)
    tell(1)
    for copy in counts:
        copy.start()

    block = min(128, width)
    whole_blocks = vocab_here // 128
    tail[pl.ds(0, vocab_here - whole_blocks * 128)] = head_v[pl.ds(whole_blocks * 128, vocab_here - whole_blocks * 128)]

    share[1].wait_recv()
    for piece, (at, size) in enumerate(PIECES):
        put(hold.at[0], at, 1, HALF + at, size)
        send_packed(snd2, 0, piece, hold[0, pl.ds(at, size)], ONE)
        packed_copy(0, 0, piece).start()
    share[3].wait_recv()
    for piece, (at, size) in enumerate(PIECES):
        put(hold.at[1], at, 3, at, size)
        send_packed(snd2, 1, piece, hold[1, pl.ds(at, size)], ONE)
        packed_copy(0, 1, piece).start()

    heard(1)
    tell(2)

    h_on.wait_recv()
    share[2].start()
    share[2].wait_recv()
    for piece, (at, size) in enumerate(PIECES):
        put(hold.at[0], at, 2, at, size)
        send_packed(snd1, 0, piece, hold[0, pl.ds(at, size)], ONE)
        packed_copy(1, 0, piece).start()
        put(hold.at[1], at, 2, HALF + at, size)
        send_packed(snd1, 1, piece, hold[1, pl.ds(at, size)], ONE)
        packed_copy(1, 1, piece).start()

    for at, size in PIECES:
        put(hold.at[0], at, 1, at, size)
        put(hold.at[1], at, 3, HALF + at, size)
    load_own.wait()
    for half in (0, HALF):
        for at, size in PIECES:
            put(logits, half + at, 0, half + at, size)

    def turn(j, carry):
        cols = pl.ds(pl.multiple_of(j * block, block), block)
        for i in range(whole_blocks):
            head_t[cols, pl.ds(i * 128, 128)] = head_v[pl.ds(i * 128, 128), cols].T
        head_t[cols, pl.ds(whole_blocks * 128, 128)] = tail[:, cols].T
        return carry

    lax.fori_loop(0, width // block, turn, 0)
    load_frozen.wait()
    for copy in load_rows[1:]:
        copy.wait()
    frozen_f[pl.ds(1184, ROWS - 1184)] = jnp.zeros((ROWS - 1184, frozen_f.shape[1]), F32)
    frozen_f[pl.ds(0, vocab_here)] = frozen_v[...].astype(F32)

    def add_into(dst, at, piece, parts):
        quarter = PIECES[piece][1] // 4
        for k, part in enumerate(parts):
            rows = pl.ds(at + k * quarter, quarter)
            dst[rows] = dst[rows] + part

    for piece, (at, size) in enumerate(PIECES):
        for slot in (0, 1):
            packed_copy(1, slot, piece).wait_recv()
            add_into(hold.at[slot], at, piece, read_packed(rcv1, slot, piece, ONE))
            send_packed(snd3, slot, piece, hold[slot, pl.ds(at, size)], TWO)
            packed_copy(2, slot, piece).start()

    heard(2)

    for slot in (0, 1):
        half = (HALF, 0)[slot]
        for piece, (at, size) in enumerate(PIECES):
            packed_copy(0, slot, piece).wait_recv()
            add_into(logits, half + at, piece, read_packed(rcv2, slot, piece, ONE))
    for piece, (at, size) in enumerate(PIECES):
        for slot in (0, 1):
            half = (0, HALF)[slot]
            packed_copy(2, slot, piece).wait_recv()
            add_into(logits, half + at, piece, read_packed(rcv3, slot, piece, TWO))

    edge = vocab_here // 8 * 8
    rows = edge + lax.broadcasted_iota(jnp.int32, (ROWS - edge, logits.shape[1]), 0)
    logits[pl.ds(edge, ROWS - edge)] = jnp.where(
        rows < vocab_here, logits[pl.ds(edge, ROWS - edge)], -1e30
    )

    step = ROWS // 4
    tops = [jnp.max(logits[pl.ds(k * step, step)], axis=0, keepdims=True) for k in range(4)]
    top = functools.reduce(jnp.maximum, tops)
    total = jnp.zeros_like(top)
    cross = jnp.zeros_like(top)
    for k in range(4):
        piece = pl.ds(k * step, step)
        shifted = jnp.exp(logits[piece] - top)
        total += jnp.sum(shifted, axis=0, keepdims=True)
        cross += jnp.sum(shifted * (logits[piece] - frozen_f[piece]), axis=0, keepdims=True)

    def far_first(i, count):
        return count // 2 + (1 - 2 * lax.rem(i, 2)) * ((i + 1) // 2)

    def exchange(top, total, cross, out, into, send, recv, to, count, meanwhile):
        out[0:1] = top
        out[1:2] = total
        out[2:3] = cross
        out[3:4] = cross

        def go(i, carry):
            k = far_first(i, count)
            remote(out, into.at[k], send.at[k], recv.at[k], to(k)).start()
            return carry

        def arrive(k, carry):
            remote(out, into.at[k], send.at[k], recv.at[k], to(k)).wait()
            return carry

        lax.fori_loop(0, count - 1, go, 0)
        meanwhile()
        lax.fori_loop(1, count, arrive, 0)
        best = top
        for k in range(1, count):
            best = jnp.maximum(best, into[k, 0:1])
        scale = jnp.exp(top - best)
        all_total, all_cross = total * scale, cross * scale
        for k in range(1, count):
            scale = jnp.exp(into[k, 0:1] - best)
            all_total += into[k, 1:2] * scale
            all_cross += into[k, 2:3] * scale
        return best, all_total, all_cross

    top_here = top
    centre = cross / total

    def early_copy(slot, kind):
        device = ((right, left)[slot], v)
        half = (slot, 1 - slot, slot)[kind]
        source = ((0, 0, 3), (0, 0, 1))[slot][kind]
        into = ((3, 3, 2), (1, 1, 2))[slot][kind]
        sem = slot * 3 + kind
        return remote(
            eu.at[source, half], eu.at[into, half], e_send.at[sem], e_recv.at[sem], device
        )

    def send_early():
        for half in (0, 1):
            for k in (0, 1):
                at = k * (EARLY // 2)
                piece = pl.ds(half * HALF + at, EARLY // 2)
                value = logits[piece]
                shifted = jnp.exp(value - top_here)
                eu[0, half, pl.ds(at, EARLY // 2)] = shifted.astype(BF16)
                eu[0, half, pl.ds(EARLY + at, EARLY // 2)] = (
                    shifted * (value - frozen_f[piece] - centre)
                ).astype(BF16)
            early_copy(half, 0).start()
        early_copy(1, 1).start()
        early_copy(0, 1).start()

    def pass_early():
        for slot in (0, 1):
            early_copy(slot, 0).wait_recv()
            early_copy(slot, 2).start()

    top, total, cross = exchange(
        top, total, cross, st1, st1_in, s1_send, s1_recv, in_group, GROUP, send_early
    )
    top, total, cross = exchange(
        top, total, cross, st2, st2_in, s2_send, s2_recv, along_z, NZ, pass_early
    )
    mean = cross / total
    out_div[...] = mean - top - jnp.log(total) + norms[...]

    for copy in counts:
        copy.wait()
    all_counts = cnt[...] + cnt_in[0] + cnt_in[1] + cnt_in[2]
    weight = cnt[...] / jnp.sum(all_counts, axis=1, keepdims=True)
    adv, ratio = advantages[...], ratios[...]
    open_ = jnp.where(adv >= 0.0, (ratio <= 1.0 + clip_eps).astype(F32), (ratio >= 1.0 - clip_eps).astype(F32))
    policy = jnp.where(open_ > 0.5, -adv * ratio, jnp.zeros_like(ratio))
    target = targets[...] - v * vocab_here
    target = jnp.where(target < vocab_here, target, -1)
    inverse = 1.0 / total
    hits = weight * policy
    terms[0:1] = weight * jnp.exp(top_here - top) * inverse
    terms[1:2] = penalty * (mean - centre) + policy
    terms[2:3] = hits
    terms[3:4] = target.astype(F32)
    tell_terms = [
        remote(terms, terms_in.at[k - 1], t_send.at[k - 1], t_recv.at[k - 1], (lax.rem(me + k, 4), v))
        for k in (1, 2, 3)
    ]
    for copy in tell_terms:
        copy.start()

    def gradient_copy(slot, kind):
        device = ((right, left)[slot], v)
        half = (slot, 1 - slot, slot)[kind]
        rows = pl.ds(half * HALF + EARLY, LATE[half])
        source = ((0, 0, 3), (0, 0, 1))[slot][kind]
        into = ((3, 3, 2), (1, 1, 2))[slot][kind]
        sem = slot * 3 + kind
        return remote(g.at[source, rows], g.at[into, rows], g_send.at[sem], g_recv.at[sem], device)

    def own_gradient(at, size):
        piece = pl.ds(at, size)
        value = logits[piece]
        chance = jnp.exp(value - top) * inverse
        rows = at + lax.broadcasted_iota(jnp.int32, value.shape, 0)
        grad = weight * (penalty * chance * (value - frozen_f[piece] - mean) - policy * chance)
        grad = jnp.where(rows == target, grad + hits, grad)
        g[0, piece] = grad.astype(BF16)

    own_gradient(EARLY, HALF - EARLY)
    gradient_copy(0, 0).start()
    own_gradient(HALF + EARLY, HALF - EARLY)
    gradient_copy(1, 0).start()
    gradient_copy(1, 1).start()
    gradient_copy(0, 1).start()
    own_gradient(0, EARLY)
    own_gradient(HALF, EARLY)

    def early_gradient(r):
        alpha, kappa, hit, there = (terms_in[3 - r, k : k + 1] for k in range(4))
        there = there.astype(jnp.int32)
        for half in (0, 1):
            for k in (0, 1):
                at = k * (EARLY // 2)
                shifted = eu[r, half, pl.ds(at, EARLY // 2)].astype(F32)
                moved = eu[r, half, pl.ds(EARLY + at, EARLY // 2)].astype(F32)
                grad = alpha * (penalty * moved - kappa * shifted)
                at = half * HALF + at
                rows = at + lax.broadcasted_iota(jnp.int32, grad.shape, 0)
                grad = jnp.where(rows == there, grad + hit, grad)
                g[r, pl.ds(at, EARLY // 2)] = grad.astype(BF16)

    chunk = width // 4
    active = lax.rem(z, 2) == core
    sender = lax.rem(z, 2) != core

    def partial(sources):
        right_side = [g[r] for r in sources]
        right_side = right_side[0] if len(sources) == 1 else jnp.concatenate(right_side, axis=1)
        deep = NZ // 8
        for i in range(4):
            value = jnp.dot(head_t[pl.ds(i * chunk, chunk)], right_side, preferred_element_type=F32)
            for j, r in enumerate(sources):
                prod[r, pl.ds(i * deep, deep)] = value[:, j * 128 : (j + 1) * 128].reshape(
                    deep, 2, NX, 16, 128
                )
        for r in sources:
            pair(r).start()

    def pair(r):
        return remote(prod.at[r, :, 1 - core], prod_in.at[r], a_send.at[r], a_recv.at[r], sibling)

    def x_copy(r, k):
        sem = r * NX + k
        return remote(xs.at[r, k], xs_in.at[r, k], x_send.at[sem], x_recv.at[sem], along_x(k))

    def z_copy(r, k):
        m = lax.rem(z // 2 + k, NZ // 2)
        there = 2 * m + core
        slot = lax.rem(z - there + NZ, NZ)
        return remote(
            zs.at[r, m], zs_in.at[r, slot], z_send.at[r * NZ + k], z_recv.at[r * NZ + slot],
            (me, there * GROUP + xc),
        )

    def to_x(r):
        pair(r).wait_recv()
        for k in (*sorted(range(1, NX), key=lambda k: -min(k, NX - k)), 0):
            there = lax.rem(x + k, NX)
            value = prod[r, :, core, there] + prod_in[r, :, there]
            if k == 0:
                mid[r] = value
            else:
                xs[r, k] = value.reshape(NZ * 8, 128).astype(BF16)
                x_copy(r, k).start()

    def to_z(r):
        value = mid[r]
        for k in range(1, NX):
            x_copy(r, k).wait_recv()
            value = value + xs_in[r, k].astype(F32).reshape(NZ // 2, 16, 128)
        mid[r] = value
        zs[r] = value.astype(BF16)

        def go(i, carry):
            z_copy(r, far_first(i, NZ // 2)).start()
            return carry

        lax.fori_loop(0, NZ // 2 - 1, go, 0)

        @pl.when(sender)
        def _():
            z_copy(r, 0).start()

    def finish(r):
        def arrive(k, carry):
            remote(
                zs.at[r, 0], zs_in.at[r, k], z_send.at[r * NZ], z_recv.at[r * NZ + k],
                (me, lax.rem(z + k, NZ) * GROUP + xc),
            ).wait_recv()
            return carry

        lax.fori_loop(1, NZ, arrive, 0)
        value = mid[r, z // 2]
        for k in range(1, NZ):
            value = value + zs_in[r, k].astype(F32)
        tokens = pl.ds(pl.multiple_of(lax.rem(me + r, 4) * 128, 128), 128)
        total_h[0, :, tokens] = value[:8]
        total_h[1, :, tokens] = value[8:]

    last = remote(
        total_h.at[1 - core], total_h.at[1 - core], f_sem.at[0], f_sem.at[1], sibling
    )

    head_rows = ((0, 304), (304, 304), (608, 304), (912, vocab_here - 912))

    def head_gradient(k):
        at, size = head_rows[k]
        rows = pl.ds(at, size)
        left_side = jnp.concatenate([g[r, rows] for r in range(4)], axis=1)
        tokens = hid[...].reshape(4 * hid.shape[1], width)
        out_head[rows] = jnp.dot(left_side, tokens, preferred_element_type=F32).astype(BF16)

    partial((0,))
    for copy in tell_terms:
        copy.wait_recv()
    gradient_copy(0, 0).wait_recv()
    gradient_copy(0, 2).start()
    gradient_copy(1, 0).wait_recv()
    gradient_copy(1, 2).start()
    to_x(0)
    for slot in (0, 1):
        early_copy(slot, 1).wait_recv()
    early_gradient(1)
    early_gradient(3)
    gradient_copy(0, 1).wait_recv()
    gradient_copy(1, 1).wait_recv()
    partial((1, 3))
    to_z(0)
    for slot in (0, 1):
        early_copy(slot, 2).wait_recv()
    early_gradient(2)
    to_x(1)
    to_x(3)
    gradient_copy(0, 2).wait_recv()
    gradient_copy(1, 2).wait_recv()
    partial((2,))
    head_gradient(0)
    to_x(2)
    to_z(1)
    to_z(3)
    head_gradient(1)
    head_gradient(2)
    to_z(2)
    head_gradient(3)

    @pl.when(active)
    def _():
        for r in (0, 1, 3, 2):
            finish(r)
        last.start()
        last.wait_send()

    @pl.when(sender)
    def _():
        last.wait_recv()

    out_hidden[...] = total_h[core].astype(BF16)

    for copy in (h_right, h_left, h_far, h_on, share[1], share[2], share[3]):
        copy.wait_send()
    for stage in range(3):
        for slot in (0, 1):
            for piece in (0, 1):
                packed_copy(stage, slot, piece).wait_send()
    for slot in (0, 1):
        for kind in range(3):
            gradient_copy(slot, kind).wait_send()
            early_copy(slot, kind).wait_send()
    for copy in tell_terms:
        copy.wait_send()
    for r in range(4):
        pair(r).wait_send()
        for k in range(1, NX):
            x_copy(r, k).wait_send()

        def left_z(k, carry):
            z_copy(r, k).wait_send()
            return carry

        lax.fori_loop(1, NZ // 2, left_z, 0)

        @pl.when(sender)
        def _():
            z_copy(r, 0).wait_send()


def local(devices, hidden, head, frozen, norms, advantages, ratios, targets, counted):
    tokens, depth = hidden.shape
    width = depth // 4
    vocab_here = head.shape[1]
    NZ = devices // (2 * NX)
    GROUP = 2 * NX
    packed = pltpu.VMEM((2, HALF // 4 * 3, tokens), jnp.int32)
    dma = pltpu.SemaphoreType.DMA
    row = [a.reshape(1, tokens) for a in (norms, advantages, ratios, targets, counted)]
    vmem = pl.BlockSpec(memory_space=pltpu.VMEM)
    out = pl.pallas_call(
        functools.partial(kernel, devices),
        out_shape=(
            jax.ShapeDtypeStruct((width // devices, 4 * tokens), BF16),
            jax.ShapeDtypeStruct((vocab_here, width), BF16),
            jax.ShapeDtypeStruct((1, tokens), F32),
        ),
        in_specs=[pl.BlockSpec(memory_space=pltpu.HBM)] * 8,
        out_specs=(vmem, vmem, vmem),
        scratch_shapes=[
            pltpu.VMEM((1, tokens), F32),
            pltpu.VMEM((1, tokens), F32),
            pltpu.VMEM((1, tokens), F32),
            pltpu.VMEM((1, tokens), jnp.int32),
            pltpu.VMEM((1, tokens), jnp.int32),
            pltpu.VMEM((vocab_here, width), BF16),
            pltpu.VMEM((width, DEEP), BF16),
            pltpu.VMEM((128, width), BF16),
            pltpu.VMEM((vocab_here, tokens), BF16),
            pltpu.VMEM((ROWS, tokens), F32),
            pltpu.VMEM((4, tokens, width), BF16),
            pltpu.VMEM((tokens // 2, width), BF16),
            pltpu.VMEM((ROWS, tokens), F32),
            pltpu.VMEM((2, HALF, tokens), F32),
            packed, packed, packed, packed, packed, packed,
            pltpu.VMEM((1, tokens), F32),
            pltpu.VMEM((3, 1, tokens), F32),
            pltpu.VMEM((4, tokens), F32),
            pltpu.VMEM((GROUP, 4, tokens), F32),
            pltpu.VMEM((4, tokens), F32),
            pltpu.VMEM((NZ, 4, tokens), F32),
            pltpu.VMEM((4, 2, 2 * EARLY, tokens), BF16),
            pltpu.VMEM((4, tokens), F32),
            pltpu.VMEM((3, 4, tokens), F32),
            pltpu.VMEM((4, DEEP, tokens), BF16),
            pltpu.VMEM((4, NZ // 2, 2, NX, 16, tokens), F32),
            pltpu.VMEM((4, NZ // 2, NX, 16, tokens), F32),
            pltpu.VMEM((4, NZ // 2, 16, tokens), F32),
            pltpu.VMEM((4, NX, NZ * 8, tokens), BF16),
            pltpu.VMEM((4, NX, NZ * 8, tokens), BF16),
            pltpu.VMEM((4, NZ // 2, 16, tokens), BF16),
            pltpu.VMEM((4, NZ, 16, tokens), BF16),
            pltpu.VMEM((2, 8, 4 * tokens), F32),
            dma((8,)),
            dma((4,)), dma((4,)),
            dma((4,)), dma((4,)),
            dma((12,)), dma((12,)),
            dma((3,)), dma((3,)),
            dma((GROUP,)), dma((GROUP,)),
            dma((NZ,)), dma((NZ,)),
            dma((6,)), dma((6,)),
            dma((3,)), dma((3,)),
            dma((6,)), dma((6,)),
            dma((4,)), dma((4,)),
            dma((4 * NX,)), dma((4 * NX,)),
            dma((4 * NZ,)), dma((4 * NZ,)),
            dma((2,)),
            pltpu.SemaphoreType.REGULAR((3,)),
        ],
        compiler_params=pltpu.CompilerParams(
            collective_id=0, has_side_effects=True, vmem_limit_bytes=48 * 1024 * 1024
        ),
    )(*(pltpu.with_memory_space_constraint(a, pltpu.HBM) for a in (hidden, head.T, frozen.T, *row)))
    return out[0].T, out[1].T, out[2].reshape(tokens)


def solution(mesh):
    return jax.shard_map(
        functools.partial(local, mesh.shape["vocab"]),
        mesh=mesh,
        in_specs=(
            P("dp", None),
            P("dp", "vocab"),
            P("dp", "vocab"),
            P("dp"),
            P("dp"),
            P("dp"),
            P("dp"),
            P("dp"),
        ),
        out_specs=(P(None, ("dp", "vocab")), P("dp", "vocab"), P("dp")),
        check_vma=False,
    )
```
